128 devices in a mesh: seq: 2 (over x_hi), dp: 64 (over z, y, x_lo, core).
Axes of the slice: x: 4 (x_hi: 2, x_lo: 2; x = x_hi * 2 + x_lo), y: 4, z: 4, core: 2. Of those that a mesh axis runs over, the one named last changes fastest.
Arguments:
- latents_in: bfloat16 [64, 256, 768], P('dp', 'seq'), may hold values from -6 to 6
- condition: bfloat16 [64, 768], P('dp'), may hold values from -6 to 6
- ada_weight: bfloat16 [1, 768, 4608], P(None, ('seq', 'dp')), may hold values from -0.21875 to 0.21875
- ada_bias: bfloat16 [1, 4608], P(None, ('seq', 'dp')), may hold values from -3 to 3
- qkv_weight: bfloat16 [1, 768, 2304], P(None, ('seq', 'dp')), may hold values from -0.21875 to 0.21875
- qv_bias: bfloat16 [1, 1536], P(None, ('seq', 'dp')), may hold values from -3 to 3
- proj_weight: bfloat16 [1, 768, 768], P(None, ('seq', 'dp')), may hold values from -0.875 to 0.875
- proj_bias: bfloat16 [1, 768], P(None, ('seq', 'dp')), may hold values from -3 to 3
- fc1_weight: bfloat16 [1, 768, 3072], P(None, ('seq', 'dp')), may hold values from -0.21875 to 0.21875
- fc1_bias: bfloat16 [1, 3072], P(None, ('seq', 'dp')), may hold values from -3 to 3
- fc2_weight: bfloat16 [1, 3072, 768], P(None, ('seq', 'dp')), may hold values from -0.109375 to 0.109375
- fc2_bias: bfloat16 [1, 768], P(None, ('seq', 'dp')), may hold values from -3 to 3
- cotangent: bfloat16 [64, 256, 768], P('dp', 'seq'), may hold values from -16 to 16
Outputs:
- latents_out: bfloat16 [64, 256, 768], P('dp', 'seq')
- latents_grad: float32 [64, 256, 768], P('dp', 'seq')
- condition_grad: float32 [64, 768], P('dp')
- ada_weight_grad: float32 [1, 768, 4608], P(None, ('seq', 'dp'))
- ada_bias_grad: float32 [1, 4608], P(None, ('seq', 'dp'))
- qkv_weight_grad: float32 [1, 768, 2304], P(None, ('seq', 'dp'))
- qv_bias_grad: float32 [1, 1536], P(None, ('seq', 'dp'))
- proj_weight_grad: float32 [1, 768, 768], P(None, ('seq', 'dp'))
- proj_bias_grad: float32 [1, 768], P(None, ('seq', 'dp'))
- fc1_weight_grad: float32 [1, 768, 3072], P(None, ('seq', 'dp'))
- fc1_bias_grad: float32 [1, 3072], P(None, ('seq', 'dp'))
- fc2_weight_grad: float32 [1, 3072, 768], P(None, ('seq', 'dp'))
- fc2_bias_grad: float32 [1, 768], P(None, ('seq', 'dp'))
The draws below stay inside these ranges and needn't reach their ends.
All inputs are finite; a program needn't handle non-finite values.
Results may differ from the reference program's by a relative error of at most 0.014.
The reference program's roundings to bfloat16 on the way count: a program that leaves them out, or rounds other values in their place, can miss the bound.
Values may be sent and summed in bfloat16 or wider, within the bound.
No kernel may reach another device: no remote copies, remote signals or barrier semaphores. Data moves between devices by JAX's collectives and lax.ppermute only.
A program may use at most 192 MiB of HBM per device.

```python
import math
import jax
import jax.numpy as jnp
from jax import lax

D = 768
HEADS = 12
HEAD_DIM = 64
FF = 3072
LEN = 256
LAYERS = 1
LATENTS = 64


def raised(values, key, source, target, blocks, factor):
    def block_of(dim):
        return (jnp.arange(values.shape[dim]) // (values.shape[dim] // blocks)).reshape((-1,) + (1,) * (values.ndim - 1 - dim))

    one_side = jax.random.permutation(key, blocks)[block_of(target)]
    far = (block_of(target) + blocks // 2) % blocks
    return jnp.where((block_of(source) == one_side) | (block_of(source) == far), factor * values, values)


def block_scale(key, shape, split, least, high):
    gain = 1.0
    for dim, shards_of in split:
        heights = jax.random.uniform(jax.random.fold_in(jax.random.fold_in(key, 6), dim), (shards_of,), jnp.float32, least / len(split), high / len(split))
        gain = gain * jnp.repeat(jnp.exp(heights), shape[dim] // shards_of).reshape((-1,) + (1,) * (len(shape) - 1 - dim))
    return gain


def gaussian(stream_key, extent, width, bound, shards=(), dtype=jnp.bfloat16):
    result = width * jax.random.normal(stream_key, extent, jnp.float32)
    if shards:
        result = result * block_scale(stream_key, extent, shards, -0.22, 0.18)
    return jnp.clip(result, -bound, bound).astype(dtype)


def heavy_noise(key, extent, spread, reach, split, heavy, held_as=jnp.bfloat16):
    result = spread * jax.random.normal(key, extent, jnp.float32)
    if split:
        result = result * block_scale(key, extent, split, -0.22, 0.18)
    return jnp.clip(raised(result, jax.random.fold_in(key, 3), *heavy), -reach, reach).astype(held_as)


def setup_inputs(seed: int = 0) -> dict:
    key_list = jax.random.split(jax.random.key(seed), 14)
    latents_in = gaussian(key_list[0], (LATENTS, LEN, D), 1.0, 6.0, ((0, 64), (1, 2)))
    condition = gaussian(key_list[1], (LATENTS, D), 1.0, 6.0, ((0, 64),))
    ada_weight = gaussian(key_list[2], (LAYERS, D, 6 * D), D ** -0.5, 0.21875, ((1, 128),))
    ada_bias = gaussian(key_list[3], (LAYERS, 6 * D), 0.5, 3.0, ((1, 128),))
    qkv_weight = gaussian(key_list[4], (LAYERS, D, 3 * D), D ** -0.5, 0.21875, ((1, 128),))
    qv_bias = gaussian(key_list[5], (LAYERS, 2 * D), 0.5, 3.0, ((1, 128),))
    proj_weight = gaussian(key_list[6], (LAYERS, D, D), (D // 16) ** -0.5, 0.875, ((1, 128),))
    proj_bias = gaussian(key_list[7], (LAYERS, D), 0.5, 3.0, ((1, 128),))
    fc1_weight = gaussian(key_list[8], (LAYERS, D, FF), D ** -0.5, 0.21875, ((1, 128),))
    fc1_bias = gaussian(key_list[9], (LAYERS, FF), 0.5, 3.0, ((1, 128),))
    fc2_weight = gaussian(key_list[10], (LAYERS, FF, D), FF ** -0.5, 0.109375, ((1, 128),))
    fc2_bias = gaussian(key_list[11], (LAYERS, D), 0.5, 3.0, ((1, 128),))
    cotangent = heavy_noise(key_list[12], (LATENTS, LEN, D), 1.0, 16.0, ((0, 64), (1, 2)), (0, 2, 64, 4.0))
    return dict(latents_in=latents_in, condition=condition, ada_weight=ada_weight, ada_bias=ada_bias, qkv_weight=qkv_weight, qv_bias=qv_bias, proj_weight=proj_weight, proj_bias=proj_bias, fc1_weight=fc1_weight, fc1_bias=fc1_bias, fc2_weight=fc2_weight, fc2_bias=fc2_bias, cotangent=cotangent)


@jax.custom_vjp
def low(v):
    return lax.optimization_barrier(v.astype(jnp.bfloat16)).astype(jnp.float32)

@jax.custom_vjp
def low_back(v):
    return v

def low_keep(v):
    return (low(v), None)

def low_pass(kept, grad):
    return (grad,)

def back_keep(v):
    return (v, None)

def back_low(kept, grad):
    return (low(grad),)
low.defvjp(low_keep, low_pass)
low_back.defvjp(back_keep, back_low)
EPSILON = 1e-06
MAX_PRECISION = lax.Precision.HIGHEST

def normalize(values):
    centre = values - lax.optimization_barrier(jnp.mean(values, axis=-1, keepdims=True))
    return centre * lax.rsqrt(lax.optimization_barrier(jnp.mean(centre * centre, axis=-1, keepdims=True)) + EPSILON)

def attend(block):
    query, keys, values = block
    scores = low_back(jnp.einsum('lqhd,lkhd->lhqk', query, keys, precision=MAX_PRECISION) * HEAD_DIM ** (-0.5))
    probs = low(jax.nn.softmax(scores, axis=-1))
    return jnp.einsum('lhqk,lkhd->lqhd', probs, values, precision=MAX_PRECISION)

def apply_layer(resid, cond_low, weights):
    ada_matrix, ada_vector, qkv_matrix, qv_vector, proj_matrix, proj_vector, up_weight, up_bias, down_weight, down_bias = weights
    latents = resid.shape[0]
    modulation = (jnp.dot(cond_low, ada_matrix, precision=MAX_PRECISION) + ada_vector).reshape(latents, 6, 1, D)
    mixed_a = low(normalize(resid) * (1.0 + modulation[:, 1]) + modulation[:, 0])
    projected = jnp.einsum('lsd,de->lse', mixed_a, qkv_matrix, precision=MAX_PRECISION)
    full_bias = jnp.concatenate([qv_vector[:D], jnp.zeros((D,), jnp.float32), qv_vector[D:]])
    projected = low_back(low(projected + full_bias))
    group = math.gcd(latents, 16)

    def blocks(piece):
        return piece.reshape(latents // group, group, LEN, HEADS, HEAD_DIM)
    attended = lax.map(jax.checkpoint(attend), (blocks(projected[..., :D]), blocks(projected[..., D:2 * D]), blocks(projected[..., 2 * D:])))
    attended = low_back(low(attended.reshape(latents, LEN, D)))
    branch_a = low_back(jnp.einsum('lsd,de->lse', attended, proj_matrix, precision=MAX_PRECISION) + proj_vector)
    middle = resid + modulation[:, 2] * branch_a
    second_mixed = low(normalize(middle) * (1.0 + modulation[:, 4]) + modulation[:, 3])
    hidden_before_act = low_back(jnp.einsum('jpi,ik->jpk', second_mixed, up_weight, precision=MAX_PRECISION) + up_bias)
    hidden_state = low(jax.nn.gelu(hidden_before_act, approximate=True))
    second_branch = low_back(jnp.einsum('zgv,vi->zgi', hidden_state, down_weight, precision=MAX_PRECISION) + down_bias)
    return middle + modulation[:, 5] * second_branch

def reference(latents_in, condition, ada_weight, ada_bias, qkv_weight, qv_bias, proj_weight, proj_bias, fc1_weight, fc1_bias, fc2_weight, fc2_bias, cotangent):
    floats = tuple((array.astype(jnp.float32) for array in (latents_in, condition, ada_weight, ada_bias, qkv_weight, qv_bias, proj_weight, proj_bias, fc1_weight, fc1_bias, fc2_weight, fc2_bias)))

    def forward(resid, cond, *params):
        cond_low = low(jax.nn.silu(cond))
        for layer_index in range(LAYERS):
            resid = apply_layer(resid, cond_low, tuple((param[layer_index] for param in params)))
        return resid
    output, pullback = jax.vjp(forward, *floats)
    grads = pullback(cotangent.astype(jnp.float32))
    return (output.astype(jnp.bfloat16), grads[0], grads[1], grads[2], grads[3], grads[4], grads[5], grads[6], grads[7], grads[8], grads[9], grads[10], grads[11])
```

```python
import jax
import jax.numpy as jnp
import numpy as np
from jax import lax
from jax.experimental import pallas as pl
from jax.experimental.pallas import tpu as pltpu
from jax.sharding import Mesh
from jax.sharding import PartitionSpec as P

HEAD_DIM = 64
EPSILON = 1e-06
BF = jnp.bfloat16
F32 = jnp.float32
SIZES = (2, 2, 2, 2, 2, 2, 2)
NAMES = ("s", "zh", "zl", "yh", "yl", "x", "c")
CHIPS = NAMES[:6]
GIVEN = ("c", "s", "zh", "yh", "zl", "yl", "x")
WIDTHS = (1664, 1536, 1536)
OUT = (
    (("s", 1, 96), ("zh", 2, 96), ("yh", 8, 48)),
    (("zh", 1, 96), ("yh", 4, 48), ("s", 1, 384)),
    (("yh", 2, 48), ("s", 1, 192), ("zh", 2, 192)),
)
COND = (("yh", 2, 48), ("zh", 1, 192))
BACK = (
    (("yh", 8, 48), ("s", 1, 192), ("zh", 1, 96)),
    (("zh", 2, 192), ("yh", 4, 48), ("s", 1, 96)),
    (("s", 1, 384), ("yh", 4, 48), ("zh", 1, 96)),
    (("zh", 2, 192), ("s", 1, 192), ("yh", 2, 48)),
    (("yh", 8, 48), ("zh", 2, 96), ("s", 1, 96)),
)
BACK_WIDTHS = (768, 896, 1024, 1024, 1024)


def bias_table():
    owners, places = [], []
    for core in range(2):
        owner, place = [], []
        for start, count, size, slot in (
            (core * 384, 384, 12, 0),
            (768 + core * 384, 384, 12, 0),
            (core * 1536, 1536, 24, 12),
            (0, 768, 6, 36),
            (0, 768, 6, 42),
        ):
            at = start + np.arange(count)
            owner.append(at // size)
            place.append(slot + at % size)
        owners.append(np.concatenate(owner))
        places.append(np.concatenate(place))
    return np.stack([np.stack(owners), np.stack(places)], axis=1).astype(np.int32)


def proj_table():
    row = np.arange(384)
    unit = row // 6 % 2 * 384 + row // 24 * 24 + row // 12 % 2 * 6 + row % 6
    return np.stack([unit, unit + 12], axis=1).astype(np.int32)


def swap(value, axis):
    return lax.ppermute(value, axis, [(0, 1), (1, 0)])


def cross(value):
    return lax.ppermute(value, ("s", "c"), [(0, 0), (1, 2), (2, 1), (3, 3)])


def pair_up(value, axis, dim):
    other = swap(value, axis)
    second = lax.axis_index(axis) == 1
    return jnp.concatenate(
        [jnp.where(second, other, value), jnp.where(second, value, other)], axis=dim
    )


def halves(first, last, axis):
    second = lax.axis_index(axis) == 1
    return jnp.where(second, last, first), jnp.where(second, first, last)


def pair_sum(value, axis, dim, send_type=F32):
    first, last = jnp.split(value, 2, axis=dim)
    mine, theirs = halves(first, last, axis)
    return mine + swap(theirs.astype(send_type), axis).astype(F32)


def exchange(value, axes):
    return lax.all_to_all(value, axes, 0, 0, tiled=True)


def cut(values, widths):
    start, parts = 0, []
    for width in widths:
        parts.append(values[..., start : start + width])
        start += width
    return parts


def bit_of(given_ref, axis):
    return given_ref[GIVEN.index(axis)] == 1


def joined_rows(given_ref, way, own_ref, came_ref, columns=slice(None)):
    axis, outer, inner = way
    second = bit_of(given_ref, axis)
    for block in range(outer):
        rows = slice(block * inner, block * inner + inner)
        own, came = own_ref[rows, columns], came_ref[rows, columns]
        yield slice(2 * block * inner, (2 * block + 1) * inner), jnp.where(second, came, own)
        yield slice((2 * block + 1) * inner, (2 * block + 2) * inner), jnp.where(second, own, came)


def split_rows(given_ref, way, value, keep_ref, send_ref):
    axis, outer, inner = way
    second = bit_of(given_ref, axis)
    for block in range(outer):
        first = value[2 * block * inner : (2 * block + 1) * inner]
        last = value[(2 * block + 1) * inner : (2 * block + 2) * inner]
        rows = slice(block * inner, block * inner + inner)
        keep_ref[rows] = jnp.where(second, last, first).astype(keep_ref.dtype)
        send_ref[rows] = jnp.where(second, first, last).astype(send_ref.dtype)


def normalize(values):
    centre = values - jnp.mean(values, axis=-1, keepdims=True)
    recip = lax.rsqrt(jnp.mean(centre * centre, axis=-1, keepdims=True) + EPSILON)
    return centre * recip, recip


def norm_back(grad_norm, normed, recip):
    return recip * (
        grad_norm
        - jnp.mean(grad_norm, axis=-1, keepdims=True)
        - normed * jnp.mean(grad_norm * normed, axis=-1, keepdims=True)
    )


def mm(left, right):
    return jnp.dot(left, right, preferred_element_type=F32)


def mm_nt(left, right):
    return lax.dot_general(left, right, (((1,), (1,)), ((), ())), preferred_element_type=F32)


def mm_tn(left, right):
    return lax.dot_general(left, right, (((0,), (0,)), ((), ())), preferred_element_type=F32)


VMEM = pl.BlockSpec(memory_space=pltpu.VMEM)


def soft_probs(query, keys):
    scores = mm_nt(query, keys) * 0.125
    raised = jnp.exp(scores - jnp.max(scores, axis=-1, keepdims=True))
    return raised / jnp.sum(raised, axis=-1, keepdims=True)


def head_cuts(qkv_ref, head):
    at = head * HEAD_DIM
    return [qkv_ref[:, base + at : base + at + HEAD_DIM] for base in (0, 384, 768)]


def call(kernel, shapes, *operands, scratch=(), later=(), room=4):
    body_of = kernel
    if later:
        count, held = len(operands), len(later)

        def body_of(*refs):
            kernel(*refs[:count], *refs[count + held :])

    arrays = [(x.shape, x.dtype) for x in operands] + list(shapes)
    held_bytes = sum(int(np.prod(size)) * jnp.dtype(kind).itemsize for size, kind in arrays)
    in_specs = [
        pl.BlockSpec(memory_space=pltpu.SMEM) if x.dtype == jnp.int32 and x.ndim == 1 else VMEM
        for x in operands
    ] + [pl.BlockSpec(memory_space=pl.ANY)] * len(later)
    return pl.pallas_call(
        body_of,
        out_shape=tuple(jax.ShapeDtypeStruct(size, kind) for size, kind in shapes),
        in_specs=in_specs,
        out_specs=(VMEM,) * len(shapes),
        scratch_shapes=scratch,
        compiler_params=pltpu.CompilerParams(vmem_limit_bytes=held_bytes + (room << 20)),
        name=getattr(kernel, "__name__", "step"),
    )(*operands, *later)


def join_parts(ways):
    def join(given_ref, *refs):
        for part, way in enumerate(ways):
            own_ref, came_ref, out_ref = refs[2 * part], refs[2 * part + 1], refs[2 * len(ways) + part]
            for rows, value in joined_rows(given_ref, way, own_ref, came_ref):
                out_ref[rows] = value

    return join


def cond_columns(given_ref, own_ref, came_ref, out_ref, rows_ref):
    for rows, value in joined_rows(given_ref, COND[1], own_ref, came_ref):
        rows_ref[rows] = value
    chip = lax.broadcasted_iota(jnp.int32, (64, 384), 0)
    latent = chip % 32 * 2 + chip // 32
    row = lax.broadcasted_iota(jnp.int32, (64, 384), 1)
    lane = lax.broadcasted_iota(jnp.int32, (128, 128), 0)
    place = lax.broadcasted_iota(jnp.int32, (128, 128), 1)
    total = jnp.zeros((64, 128), F32)
    for tile in range(6):
        values = mm(one_hot(row, 6 * latent + tile), rows_ref[...]).astype(BF)
        wanted = jnp.where(place < 6, given_ref[len(GIVEN)] * 6 + place - 128 * tile, -1)
        total += mm(values, one_hot(lane, wanted))
    out_ref[...] = total.astype(BF)


def split_parts(ways):
    def split(given_ref, *refs):
        count = len(ways)
        for part, way in enumerate(ways):
            value = refs[2 * part][...].astype(F32) + refs[2 * part + 1][...].astype(F32)
            split_rows(
                given_ref, way, value, refs[2 * count + 2 * part], refs[2 * count + 2 * part + 1]
            )

    return split


def split_all(given_ref, *refs):
    keep_ref, send_ref = refs[10], refs[11]
    at = 0
    for part, width in enumerate(BACK_WIDTHS):
        columns = slice(at, at + width)
        value = refs[2 * part][...] + refs[2 * part + 1][...].astype(F32)
        split_rows(given_ref, ("zl", 1, 48), value, keep_ref.at[:, columns], send_ref.at[:, columns])
        at += width


def split_last(given_ref, keep_ref, came_ref, near_keep, near_send, far_keep, far_send):
    value = keep_ref[...] + came_ref[...].astype(F32)
    second = bit_of(given_ref, "x")
    for columns, at in ((slice(0, 1152), 0), (slice(1664, 3200), 1152), (slice(1536, 1664), 2688)):
        first, last = value[:12, columns], value[12:, columns]
        to = slice(at, at + first.shape[1])
        near_keep[:, to] = jnp.where(second, last, first)
        near_send[:, to] = jnp.where(second, first, last)
    first, last = value[:, 3200:3968], value[:, 3968:]
    far_keep[:24] = jnp.where(second, last, first)
    far_send[:24] = jnp.where(second, first, last)
    for half in range(2):
        first, last = [value[12 * half + x : 12 * half + x + 6, 1152:1536] for x in (0, 6)]
        to = slice(384 * half, 384 * half + 384)
        far_keep[24:, to] = jnp.where(second, last, first)
        far_send[24:, to] = jnp.where(second, first, last)


def split_cores(given_ref, keep_ref, came_ref, far_ref, far_came_ref, near_keep, near_send, down_ref, proj_ref):
    value = keep_ref[...] + came_ref[...]
    second = bit_of(given_ref, "c")
    near_keep[...] = jnp.where(second, value[6:], value[:6])
    near_send[...] = jnp.where(second, value[:6], value[6:])
    far = far_ref[...] + far_came_ref[...]
    down_ref[...] = far[:24]
    proj_ref[...] = far[24:]


def ada_grads(core_ref, mod_ref, cond_ref, rows_ref, keep_ref, send_ref, term_ref, sums_ref):
    mods = mod_ref[...].astype(F32)
    mods = jnp.concatenate([mods[:, row, :] for row in range(18)], axis=1).astype(BF)
    pair = mm_tn(cond_ref[...], mods)
    second = bit_of(core_ref, "c")
    keep_ref[...] = jnp.where(second, pair[6:], pair[:6])
    send_ref[...] = jnp.where(second, pair[:6], pair[6:])
    term_ref[...] = mm_nt(mods, rows_ref[...])
    sums_ref[...] = column_sum(mods.astype(F32))


def one_hot(index, at):
    return (index == at).astype(F32).astype(BF)


def row_picks():
    row = lax.broadcasted_iota(jnp.int32, (768, 128), 0)
    device = lax.broadcasted_iota(jnp.int32, (768, 128), 1)
    return one_hot(row, 6 * device)


def bias_vector(units, table_ref):
    rows = mm_tn(row_picks(), units).astype(BF)
    index = lax.broadcasted_iota(jnp.int32, (128, 3840), 0)
    picked = mm_tn(rows, one_hot(index, table_ref[0:1]))
    return column_sum(jnp.where(index == table_ref[1:2], picked, 0.0))


def bias_units(vector, table_ref):
    index = lax.broadcasted_iota(jnp.int32, (128, 3840), 0)
    spread_out = jnp.where(index == table_ref[0:1], vector, 0.0).astype(BF)
    rows = mm_nt(spread_out, one_hot(index, table_ref[1:2])).astype(BF)
    return mm(row_picks(), rows)


def mod_add(keep_ref, came_ref, out_ref):
    total = keep_ref[...] + came_ref[...]
    for row in range(18):
        out_ref[:, row, :] = total[:, 128 * row : 128 * row + 128]


def mod_sum(got_ref, out_ref):
    total = jnp.sum(got_ref[...], axis=0)
    for row in range(18):
        at = 128 * (row % 6)
        out_ref[row // 6 : row // 6 + 1, at : at + 128] = total[row : row + 1]


def mod_grads(core_ref, start_ref, middle_ref, out_ref, keep_ref, send_ref):
    first = jnp.concatenate([start_ref[...], middle_ref[0:1]], axis=0)
    last = jnp.concatenate([middle_ref[1:3], out_ref[0:1]], axis=0)
    second = core_ref[0] == 1
    keep_ref[...] = jnp.where(second, last, first)
    send_ref[...] = jnp.where(second, first, last)


def mod_join(keep_ref, came_ref, out_ref):
    total = keep_ref[...] + came_ref[...]
    rows = [
        total[row // 6 : row // 6 + 1, 128 * (row % 6) : 128 * (row % 6) + 128] for row in range(18)
    ]
    out_ref[...] = jnp.broadcast_to(jnp.concatenate(rows, axis=0)[None], (64, 18, 128)).astype(BF)


def owners(core_ref, keep_ref, came_ref, qkv_ref, qv_ref, proj_ref, up_ref, up_bias_ref, down_ref):
    keep, came = keep_ref[...], came_ref[...]
    second = core_ref[0] == 1
    left, right = jnp.where(second, came, keep), jnp.where(second, keep, came)
    for part in range(3):
        from_ = slice(384 * part, 384 * part + 384)
        for row in range(6):
            qkv_ref[row, :, 768 * part : 768 * part + 384] = left[row : row + 1, from_]
            qkv_ref[row, :, 768 * part + 384 : 768 * part + 768] = right[row : row + 1, from_]
    for row in range(6):
        up_ref[row, :, :1536] = left[row : row + 1, 1152:2688]
        up_ref[row, :, 1536:] = right[row : row + 1, 1152:2688]
    sums = (keep + came)[0:1, 2688:]
    qv_ref[...] = sums[:, :12]
    up_bias_ref[...] = sums[:, 12:36]
    proj_ref[...] = sums[:, 36:42]
    down_ref[...] = sums[:, 42:48]


def part_ways(core_ref, value, keep_ref, send_ref):
    second = core_ref[0] == 1
    keep_ref[...] = jnp.where(second, value[128:], value[:128])
    send_ref[...] = jnp.where(second, value[:128], value[128:])


def modulate(normed, mod_ref, shift):
    return (normed * (1.0 + mod_ref[shift + 1 : shift + 2]) + mod_ref[shift : shift + 1]).astype(BF)


def column_sum(value):
    return jnp.sum(value, axis=0, keepdims=True)


def first_mix(x_ref, mod_ref, mixed_ref):
    normed, _ = normalize(x_ref[...].astype(F32))
    mixed_ref[...] = modulate(normed, mod_ref, 0)


def attend(
    core_ref, mixed_ref, own_ref, came_ref, bias_table_ref, table_ref,
    bias_ref, weight_ref, qkv_ref, attended_ref, proj_ref, keep_ref, send_ref,
):
    for rows, value in joined_rows(core_ref, OUT[0][2], own_ref, came_ref):
        weight_ref[rows] = value
    bias_ref[...] = bias_vector(weight_ref[:, 1536:], bias_table_ref)
    projected = mm(mixed_ref[...], weight_ref[:, :1152])
    qkv_ref[:, :384] = (projected[:, :384] + bias_ref[:, :384]).astype(BF)
    qkv_ref[:, 384:768] = projected[:, 384:768].astype(BF)
    qkv_ref[:, 768:] = (projected[:, 768:] + bias_ref[:, 384:768]).astype(BF)
    units = weight_ref[:, 1152:1536]
    index = lax.broadcasted_iota(jnp.int32, (384, 768), 1)
    for half in range(2):
        picks = one_hot(index, table_ref[:, half : half + 1])
        proj_ref[:, 384 * half : 384 * half + 384] = mm(picks, units).astype(BF)
    for head in range(6):
        query, keys, values = head_cuts(qkv_ref, head)
        probs = soft_probs(query, keys).astype(BF)
        at = head * HEAD_DIM
        attended_ref[:, at : at + HEAD_DIM] = mm(probs, values).astype(BF)
    part_ways(core_ref, mm(attended_ref[...], proj_ref[...]), keep_ref, send_ref)


def second_mix(keep_ref, came_ref, bias_ref, x_ref, mod_ref, branch_ref, middle_ref, mixed_ref):
    branch = keep_ref[...] + came_ref[...] + bias_ref[:, 2304:3072]
    middle = x_ref[...].astype(F32) + mod_ref[2:3] * branch
    normed, _ = normalize(middle)
    branch_ref[...] = branch
    middle_ref[...] = middle
    mixed_ref[...] = modulate(normed, mod_ref, 3)


def down_rows(pair, half):
    return [(2 * pair + side) * 96 + half * 48 for side in range(2)]


def feed(
    core_ref, mixed_ref, grad_ref, bias_ref, up_own_ref, up_came_ref, own_ref, came_ref,
    keep_ref, send_ref, back_keep_ref, back_send_ref,
    a_keep_ref, a_send_ref, b_keep_ref, b_send_ref, c_keep_ref, c_send_ref, sums_ref,
    hidden_ref, slope_ref, down_ref, up_ref, units_ref,
):
    for rows, value in joined_rows(core_ref, OUT[1][2], up_own_ref, up_came_ref):
        up_ref[rows] = value
    for rows, value in joined_rows(core_ref, OUT[2][2], own_ref, came_ref):
        units_ref[rows] = value
    mixed, grad = mixed_ref[...], grad_ref[...]
    for at in range(0, 1536, 512):
        pre = mm(mixed, up_ref[:, at : at + 512]) + bias_ref[:, 768 + at : 1280 + at]
        square = pre * pre
        tanh = jnp.tanh(0.7978845608028654 * pre * (1.0 + 0.044715 * square))
        half = 0.5 * (1.0 + tanh)
        hidden_ref[:, at : at + 512] = (pre * half).astype(BF)
        slope_ref[:, at : at + 512] = half + 0.5 * pre * (1.0 - tanh * tanh) * (
            0.7978845608028654 * (1.0 + 3.0 * 0.044715 * square)
        )
    for pair in range(8):
        for half in range(2):
            columns = slice(half * 768, half * 768 + 768)
            near = units_ref[48 * pair : 48 * pair + 48, columns].astype(F32)
            far = units_ref[384 + 48 * pair : 432 + 48 * pair, columns].astype(F32)
            for side, row in enumerate(down_rows(pair, half)):
                cut_ = slice(24 * side, 24 * side + 24)
                down_ref[row : row + 48] = jnp.concatenate([near[cut_], far[cut_]]).astype(BF)
    hidden, down = hidden_ref[...], down_ref[...]
    grad_pre = (mm_nt(grad, down) * slope_ref[...]).astype(BF)
    part_ways(core_ref, mm_nt(grad_pre, up_ref[...]), back_keep_ref, back_send_ref)
    part_ways(core_ref, mm(hidden, down), keep_ref, send_ref)
    grad_up = mm_tn(mixed, grad_pre)
    split_rows(core_ref, BACK[2][0], grad_up[:, :1024], a_keep_ref, a_send_ref)
    grad_down = mm_tn(hidden, grad)
    for pair in range(8):
        for half in range(2):
            columns = slice(half * 768, half * 768 + 768)
            for side in range(2):
                units_ref[384 * side + 48 * pair : 384 * side + 48 * pair + 48, columns] = jnp.concatenate(
                    [grad_down[r + 24 * side : r + 24 * side + 24] for r in down_rows(pair, half)]
                ).astype(BF)
    left, right = slice(0, 512), slice(512, 1024)
    split_rows(core_ref, BACK[3][0], grad_up[:, 1024:], b_keep_ref.at[:, left], b_send_ref.at[:, left])
    split_rows(core_ref, BACK[3][0], units_ref[:, :512], b_keep_ref.at[:, right], b_send_ref.at[:, right])
    split_rows(core_ref, BACK[4][0], units_ref[:, 512:], c_keep_ref, c_send_ref)
    sums_ref[...] = column_sum(grad_pre.astype(F32))


def finish(keep_ref, came_ref, bias_ref, middle_ref, grad_ref, mod_ref, out_ref, sums_ref):
    branch = keep_ref[...] + came_ref[...] + bias_ref[:, 3072:3840]
    out_ref[...] = (middle_ref[...] + mod_ref[5:6] * branch).astype(BF)
    grad = grad_ref[...].astype(F32)
    sums_ref[0:1] = column_sum(grad * branch)
    sums_ref[1:2] = column_sum((mod_ref[5:6] * grad).astype(BF).astype(F32))


def middle_back(
    keep_ref, came_ref, middle_ref, branch_ref, grad_ref, mod_ref, grad_middle_ref, grad_branch_ref, sums_ref
):
    grad_mixed = keep_ref[...] + came_ref[...]
    normed, recip = normalize(middle_ref[...])
    grad_middle = grad_ref[...].astype(F32) + norm_back(
        grad_mixed * (1.0 + mod_ref[4:5]), normed, recip
    )
    grad_branch = (mod_ref[2:3] * grad_middle).astype(BF)
    grad_middle_ref[...] = grad_middle
    grad_branch_ref[...] = grad_branch
    sums_ref[0:1] = column_sum(grad_middle * branch_ref[...])
    sums_ref[1:2] = column_sum(grad_mixed)
    sums_ref[2:3] = column_sum(grad_mixed * normed)
    sums_ref[3:4] = column_sum(grad_branch.astype(F32))


def attend_back(
    core_ref, grad_ref, proj_ref, qkv_ref, attended_ref, mixed_ref, weight_ref,
    table_ref, bias_table_ref, up_sums_ref, middle_sums_ref, out_sums_ref,
    keep_ref, send_ref, one_keep_ref, one_send_ref, two_keep_ref, two_send_ref, grad_qkv_ref,
):
    grad = grad_ref[...]
    grad_attended = mm_nt(grad, proj_ref[...]).astype(BF)
    for head in range(6):
        query, keys, values = head_cuts(qkv_ref, head)
        at = head * HEAD_DIM
        grad_out = grad_attended[:, at : at + HEAD_DIM]
        probs = soft_probs(query, keys)
        grad_probs = mm_nt(grad_out, values)
        total = jnp.sum(probs * grad_probs, axis=-1, keepdims=True)
        grad_scores = (probs * (grad_probs - total)).astype(BF)
        grad_qkv_ref[:, at : at + HEAD_DIM] = (mm(grad_scores, keys) * 0.125).astype(BF)
        at += 384
        grad_qkv_ref[:, at : at + HEAD_DIM] = (mm_tn(grad_scores, query) * 0.125).astype(BF)
        at += 384
        grad_qkv_ref[:, at : at + HEAD_DIM] = mm_tn(probs.astype(BF), grad_out).astype(BF)
    grad_qkv = grad_qkv_ref[...]
    part_ways(core_ref, mm_nt(grad_qkv, weight_ref[:, :1152]), keep_ref, send_ref)
    one = mm_tn(mixed_ref[...], grad_qkv[:, :768])
    split_rows(core_ref, BACK[0][0], one, one_keep_ref, one_send_ref)
    grad_proj = mm_tn(attended_ref[...], grad).astype(BF)
    index = lax.broadcasted_iota(jnp.int32, (384, 768), 1)
    units = jnp.zeros((768, 384), F32)
    for half in range(2):
        picks = one_hot(index, table_ref[:, half : half + 1])
        units += mm_tn(picks, grad_proj[:, 384 * half : 384 * half + 384])
    sums = column_sum(grad_qkv.astype(F32))
    vector = jnp.concatenate(
        [sums[:, :384], sums[:, 768:], up_sums_ref[...], middle_sums_ref[3:4], out_sums_ref[1:2]], axis=1
    )
    two = jnp.concatenate(
        [mm_tn(mixed_ref[...], grad_qkv[:, 768:]), units, bias_units(vector, bias_table_ref)], axis=1
    )
    split_rows(core_ref, BACK[1][0], two, two_keep_ref, two_send_ref)


def start_back(keep_ref, came_ref, x_ref, grad_middle_ref, mod_ref, grad_ref, sums_ref):
    grad_mixed = keep_ref[...] + came_ref[...]
    normed, recip = normalize(x_ref[...].astype(F32))
    grad_ref[...] = grad_middle_ref[...] + norm_back(
        grad_mixed * (1.0 + mod_ref[1:2]), normed, recip
    )
    sums_ref[0:1] = column_sum(grad_mixed)
    sums_ref[1:2] = column_sum(grad_mixed * normed)


def body(
    latents_in,
    condition,
    ada_weight,
    ada_bias,
    qkv_weight,
    qv_bias,
    proj_weight,
    proj_bias,
    fc1_weight,
    fc1_bias,
    fc2_weight,
    fc2_bias,
    cotangent,
):
    core = lax.axis_index("c")
    at_s = lax.axis_index("s")
    cond = condition.astype(F32)
    cond_low = jax.nn.silu(cond).astype(BF)

    qkv_cut = qkv_weight[0].reshape(6, 3, 2, 384)
    bias_row = jnp.concatenate([qv_bias, fc1_bias, proj_bias, fc2_bias], axis=1)
    bias_tile = jnp.pad(bias_row, ((0, 5), (0, 128 - 48)))
    first = jnp.concatenate([qkv_cut[:, :, 0].reshape(6, 1152), fc1_weight[0, :, :1536]], axis=1)
    last = jnp.concatenate([qkv_cut[:, :, 1].reshape(6, 1152), fc1_weight[0, :, 1536:]], axis=1)
    mine, theirs = halves(first, last, "c")
    tiles = jnp.concatenate([bias_tile, cond_low.reshape(6, 128)], axis=1)
    mine = jnp.concatenate([mine, tiles], axis=1)
    theirs = jnp.concatenate([theirs, tiles], axis=1)
    other = swap(theirs, "c")
    second = core == 1
    unit12 = jnp.concatenate(
        [jnp.where(second, other, mine), jnp.where(second, mine, other)], axis=0
    )
    unit24 = pair_up(unit12, "x", 0)
    crossed = cross(jnp.concatenate([fc2_weight[0], proj_weight[0]], axis=0))
    crossed = pair_up(crossed[None], "x", 0)
    proj_unit = crossed[:, 24:].reshape(2, 6, 2, 384).transpose(2, 0, 1, 3).reshape(24, 384)
    unit = jnp.concatenate(
        [unit24[:, :1152], proj_unit, unit24[:, 2688:2816], unit24[:, 1152:2688], crossed[0, :24], crossed[1, :24], unit24[:, 2816:]],
        axis=1,
    )
    near = pair_up(pair_up(unit[None], "yl", 0)[None], "zl", 0).reshape(96, 4864)

    which = jnp.stack([lax.axis_index(a) for a in (*GIVEN, NAMES)]).astype(jnp.int32)

    def step_out(parts, ways):
        pairs = [x for p, way in zip(parts, ways) for x in (p, swap(p, way[0]))]
        shapes = [((p.shape[0] * 2, p.shape[1]), BF) for p in parts]
        return call(join_parts(ways), shapes, which, *pairs)

    *parts, conds = step_out(cut(near, (*WIDTHS, 128)), [*(way[0] for way in OUT), COND[0]])
    (cond_cols,) = call(
        cond_columns, [((64, 128), BF)], which, conds, swap(conds, "zh"),
        scratch=[pltpu.VMEM((384, 128), BF)],
    )
    cond_cols = cond_cols[:, :6]
    pair_cond = pair_up(cond_cols, "c", 1)

    device = lax.axis_index(NAMES)
    own_bias = lax.dynamic_update_slice(jnp.zeros((4608,), F32), ada_bias[0].astype(F32), (device * 36,))
    partial = mm(cond_cols, ada_weight[0]) + own_bias
    keep, send = halves(partial[:, :2304], partial[:, 2304:], "c")
    parts = step_out(parts, [way[1] for way in OUT])
    (partial,) = call(mod_add, [((64, 18, 128), F32)], keep, swap(send, "c"), later=tuple(parts))
    mod_parts = exchange(partial, CHIPS)
    (mod_half,) = call(mod_sum, [((3, 768), F32)], mod_parts)
    modulation = lax.all_gather(mod_half, "c", axis=0, tiled=True)

    one_own, up_own, units_own = parts
    one_came, up_came, units_came = [swap(p, way[2][0]) for p, way in zip(parts, OUT)]

    proj_rows = jnp.asarray(proj_table())
    bias_places = lax.dynamic_index_in_dim(jnp.asarray(bias_table()), core, 0, False)
    resid, grad_out = cross(latents_in[0]), cross(cotangent[0])
    own = ((128, 768), F32)
    own_low = ((128, 768), BF)
    (mixed_a,) = call(first_mix, [own_low], resid, modulation)
    mixed_a = lax.all_gather(mixed_a, "c", axis=0, tiled=True)
    own_gbb = (modulation[5:6] * grad_out.astype(F32)).astype(BF)
    grad_branch_b = lax.all_gather(own_gbb, "c", axis=0, tiled=True)
    biases, weight_one, qkv, attended, proj_half, keep, send = call(
        attend,
        [((1, 3840), F32), ((768, 1664), BF), ((256, 1152), BF), ((256, 384), BF), ((384, 768), BF), own, own],
        which, mixed_a, one_own, one_came, bias_places, proj_rows,
        room=10,
        later=(grad_branch_b,),
    )
    branch_a, middle, mixed_b = call(
        second_mix, [own, own, own_low], keep, swap(send, "c"), biases, resid, modulation
    )
    mixed_b = lax.all_gather(mixed_b, "c", axis=0, tiled=True)
    out_keep, out_send, keep, send, *feed_parts, up_sums = call(
        feed,
        [own] * 4 + [((384, 1024), BF)] * 6 + [((1, 1536), F32)],
        which, mixed_b, grad_branch_b, biases, up_own, up_came, units_own, units_came,
        scratch=[
            pltpu.VMEM((256, 1536), BF),
            pltpu.VMEM((256, 1536), F32),
            pltpu.VMEM((1536, 768), BF),
            pltpu.VMEM((768, 1536), BF),
            pltpu.VMEM((768, 1536), BF),
        ],
        room=30,
    )
    grad_middle, own_gba, middle_sums = call(
        middle_back,
        [own, own_low, ((4, 768), F32)],
        keep, swap(send, "c"), middle, branch_a, grad_out, modulation,
    )
    grad_branch_a = lax.all_gather(own_gba, "c", axis=0, tiled=True)
    output, out_sums = call(
        finish,
        [own_low, ((2, 768), F32)],
        out_keep, swap(out_send, "c"), biases, middle, grad_out, modulation,
    )
    def step_back(parts, chosen, step, later=()):
        pairs = [x for (k, v), i in zip(parts, chosen) for x in (k, swap(v, BACK[i][step][0]))]
        rows = 192 // (step + 1)
        shapes = [((rows, BACK_WIDTHS[i]), kind) for i in chosen for kind in (F32, BF)]
        ways = [BACK[i][step + 1] for i in chosen]
        done = call(split_parts(ways), shapes, which, *pairs, later=later)
        return list(zip(done[::2], done[1::2]))

    feed_parts = list(zip(feed_parts[::2], feed_parts[1::2]))
    feed_parts = step_back(feed_parts, (2, 3, 4), 0)
    keep, send, one_keep, one_send, two_keep, two_send = call(
        attend_back,
        [own, own] + [((384, 768), BF)] * 2 + [((384, 896), BF)] * 2,
        which, grad_branch_a, proj_half, qkv, attended, mixed_a, weight_one,
        proj_rows, bias_places, up_sums, middle_sums, out_sums,
        scratch=[pltpu.VMEM((256, 1152), BF)],
        room=20,
    )
    grad_resid, start_sums = call(
        start_back,
        [own, ((2, 768), F32)],
        keep, swap(send, "c"), resid, grad_middle, modulation,
        later=feed_parts[0],
    )

    ada_keep, ada_give = halves(ada_weight[0, :, :2304], ada_weight[0, :, 2304:], "c")
    ada_came = swap(ada_give, "c")
    second = core == 1
    ada_rows = jnp.concatenate(
        [jnp.where(second, ada_came, ada_keep), jnp.where(second, ada_keep, ada_came)], axis=0
    )
    keep, send = call(
        mod_grads, [((3, 768), F32)] * 2, which, start_sums, middle_sums, out_sums
    )
    (grad_mod,) = call(mod_join, [((64, 18, 128), BF)], keep, swap(send, "c"))
    all_mod = exchange(grad_mod, CHIPS)
    keep, give, term, sums = call(
        ada_grads,
        [((6, 2304), F32)] * 2 + [((64, 12), F32), ((1, 2304), F32)],
        which, all_mod, pair_cond, ada_rows,
    )
    came = swap(give, "c")
    grad_ada = jnp.concatenate(
        [jnp.where(second, came, keep), jnp.where(second, keep, came)], axis=1
    )[None]
    ada_sums = jnp.where(core == at_s, sums, swap(sums, "c"))
    grad_ada_bias = lax.dynamic_slice_in_dim(ada_sums, device % 64 * 36, 36, 1)
    term = term.reshape(2, 32, 12).transpose(1, 0, 2).reshape(32, 24)
    term = exchange(jnp.concatenate([term, term], axis=0), CHIPS)
    term = term.reshape(64, 2, 12).transpose(1, 0, 2).reshape(2, 768)

    far_one = [(one_keep, one_send), (two_keep, two_send)]
    far_one = step_back(far_one, (0, 1), 0)
    feed_parts = step_back(feed_parts, (2, 3, 4), 1)
    far_two = step_back(far_one, (0, 1), 1, (feed_parts[0][0], all_mod))
    pairs = [x for (k, v), way in zip(far_two + feed_parts, BACK) for x in (k, swap(v, way[2][0]))]
    keep, send = call(
        split_all, [((48, 4736), F32), ((48, 4736), BF)], which, *pairs
    )
    latents_grad, output = cross(grad_resid), cross(output)
    keep, send = call(
        split_parts([("yl", 1, 24)]), [((24, 4736), F32), ((24, 4736), BF)], which, keep, swap(send, "zl")
    )
    near_keep, near_send, far_keep, far_send = call(
        split_last,
        [((12, 2816), F32)] * 2 + [((30, 768), F32)] * 2,
        which, keep, swap(send, "yl"),
        later=(latents_grad, output),
    )
    keep, send, down, proj = call(
        split_cores,
        [((6, 2816), F32)] * 2 + [((24, 768), F32), ((6, 768), F32)],
        which, near_keep, swap(near_send, "x"), far_keep, swap(far_send, "x"),
    )
    grad_fc2, grad_proj = cross(down)[None], cross(proj)[None]
    grad_qkv, grad_qv, grad_proj_bias, grad_fc1, grad_fc1_bias, grad_fc2_bias = call(
        owners,
        [((6, 1, 2304), F32), ((1, 12), F32), ((1, 6), F32), ((6, 1, 3072), F32), ((1, 24), F32), ((1, 6), F32)],
        which, keep, swap(send, "c"),
    )

    cond_sum = pair_sum(term, "c", 0)
    sigmoid = jax.nn.sigmoid(cond)
    cond_grad = cond_sum * (sigmoid * (1.0 + cond * (1.0 - sigmoid)))

    return (
        output[None],
        latents_grad[None],
        cond_grad,
        grad_ada,
        grad_ada_bias,
        grad_qkv.reshape(1, 6, 2304),
        grad_qv,
        grad_proj,
        grad_proj_bias,
        grad_fc1.reshape(1, 6, 3072),
        grad_fc1_bias,
        grad_fc2,
        grad_fc2_bias,
    )


def solution(mesh):
    finer = Mesh(mesh.devices.reshape(SIZES), NAMES)
    tokens = P(NAMES[1:], "s", None)
    cond = P(NAMES[1:], None)
    matrix = P(None, NAMES, None)
    vector = P(None, NAMES)
    weights = (matrix, vector) * 5
    return jax.shard_map(
        body,
        mesh=finer,
        in_specs=(tokens, cond) + weights + (tokens,),
        out_specs=(tokens, tokens, cond) + weights,
        check_vma=False,
    )
```

```python
import jax
import jax.numpy as jnp
import numpy as np
from jax import lax
from jax.experimental import pallas as pl
from jax.experimental.pallas import tpu as pltpu
from jax.sharding import Mesh
from jax.sharding import PartitionSpec as P

HEAD_DIM = 64
EPSILON = 1e-06
BF = jnp.bfloat16
F32 = jnp.float32
SIZES = (2, 2, 2, 2, 2, 2, 2)
NAMES = ("s", "zh", "zl", "yh", "yl", "x", "c")
CHIPS = NAMES[:6]
GIVEN = ("c", "s", "zh", "yh", "zl", "yl", "x")
WIDTHS = (1664, 1536, 1536)
OUT = (
    (("s", 1, 96), ("zh", 2, 96), ("yh", 8, 48)),
    (("zh", 1, 96), ("yh", 4, 48), ("s", 1, 384)),
    (("yh", 2, 48), ("s", 1, 192), ("zh", 2, 192)),
)
COND = (("yh", 2, 48), ("zh", 1, 192))
BACK = (
    (("yh", 8, 48), ("s", 1, 192), ("zh", 1, 96)),
    (("zh", 2, 192), ("yh", 4, 48), ("s", 1, 96)),
    (("s", 1, 384), ("yh", 4, 48), ("zh", 1, 96)),
    (("zh", 2, 192), ("s", 1, 192), ("yh", 2, 48)),
    (("yh", 8, 48), ("zh", 2, 96), ("s", 1, 96)),
)
BACK_WIDTHS = (768, 896, 1024, 1024, 1024)


def bias_table():
    owners, places = [], []
    for core in range(2):
        owner, place = [], []
        for start, count, size, slot in (
            (core * 384, 384, 12, 0),
            (768 + core * 384, 384, 12, 0),
            (core * 1536, 1536, 24, 12),
            (0, 768, 6, 36),
            (0, 768, 6, 42),
        ):
            at = start + np.arange(count)
            owner.append(at // size)
            place.append(slot + at % size)
        owners.append(np.concatenate(owner))
        places.append(np.concatenate(place))
    return np.stack([np.stack(owners), np.stack(places)], axis=1).astype(np.int32)


def proj_table():
    row = np.arange(384)
    unit = row // 6 % 2 * 384 + row // 24 * 24 + row // 12 % 2 * 6 + row % 6
    return np.stack([unit, unit + 12], axis=1).astype(np.int32)


def swap(value, axis):
    return lax.ppermute(value, axis, [(0, 1), (1, 0)])


def cross(value):
    return lax.ppermute(value, ("s", "c"), [(0, 0), (1, 2), (2, 1), (3, 3)])


def pair_up(value, axis, dim):
    other = swap(value, axis)
    second = lax.axis_index(axis) == 1
    return jnp.concatenate(
        [jnp.where(second, other, value), jnp.where(second, value, other)], axis=dim
    )


def halves(first, last, axis):
    second = lax.axis_index(axis) == 1
    return jnp.where(second, last, first), jnp.where(second, first, last)


def pair_sum(value, axis, dim, send_type=F32):
    first, last = jnp.split(value, 2, axis=dim)
    mine, theirs = halves(first, last, axis)
    return mine + swap(theirs.astype(send_type), axis).astype(F32)


def exchange(value, axes):
    return lax.all_to_all(value, axes, 0, 0, tiled=True)


def cut(values, widths):
    start, parts = 0, []
    for width in widths:
        parts.append(values[..., start : start + width])
        start += width
    return parts


def bit_of(given_ref, axis):
    return given_ref[GIVEN.index(axis)] == 1


def joined_rows(given_ref, way, own_ref, came_ref, columns=slice(None)):
    axis, outer, inner = way
    second = bit_of(given_ref, axis)
    for block in range(outer):
        rows = slice(block * inner, block * inner + inner)
        own, came = own_ref[rows, columns], came_ref[rows, columns]
        yield slice(2 * block * inner, (2 * block + 1) * inner), jnp.where(second, came, own)
        yield slice((2 * block + 1) * inner, (2 * block + 2) * inner), jnp.where(second, own, came)


def split_rows(given_ref, way, value, keep_ref, send_ref):
    axis, outer, inner = way
    second = bit_of(given_ref, axis)
    for block in range(outer):
        first = value[2 * block * inner : (2 * block + 1) * inner]
        last = value[(2 * block + 1) * inner : (2 * block + 2) * inner]
        rows = slice(block * inner, block * inner + inner)
        keep_ref[rows] = jnp.where(second, last, first).astype(keep_ref.dtype)
        send_ref[rows] = jnp.where(second, first, last).astype(send_ref.dtype)


def normalize(values):
    centre = values - jnp.mean(values, axis=-1, keepdims=True)
    recip = lax.rsqrt(jnp.mean(centre * centre, axis=-1, keepdims=True) + EPSILON)
    return centre * recip, recip


def norm_back(grad_norm, normed, recip):
    return recip * (
        grad_norm
        - jnp.mean(grad_norm, axis=-1, keepdims=True)
        - normed * jnp.mean(grad_norm * normed, axis=-1, keepdims=True)
    )


def mm(left, right):
    return jnp.dot(left, right, preferred_element_type=F32)


def mm_nt(left, right):
    return lax.dot_general(left, right, (((1,), (1,)), ((), ())), preferred_element_type=F32)


def mm_tn(left, right):
    return lax.dot_general(left, right, (((0,), (0,)), ((), ())), preferred_element_type=F32)


VMEM = pl.BlockSpec(memory_space=pltpu.VMEM)


def soft_probs(query, keys):
    scores = mm_nt(query, keys) * 0.125
    raised = jnp.exp(scores - jnp.max(scores, axis=-1, keepdims=True))
    return raised / jnp.sum(raised, axis=-1, keepdims=True)


def head_cuts(qkv_ref, head):
    at = head * HEAD_DIM
    return [qkv_ref[:, base + at : base + at + HEAD_DIM] for base in (0, 384, 768)]


def call(kernel, shapes, *operands, scratch=(), later=(), room=4):
    body_of = kernel
    if later:
        count, held = len(operands), len(later)

        def body_of(*refs):
            kernel(*refs[:count], *refs[count + held :])

    arrays = [(x.shape, x.dtype) for x in operands] + list(shapes)
    held_bytes = sum(int(np.prod(size)) * jnp.dtype(kind).itemsize for size, kind in arrays)
    in_specs = [
        pl.BlockSpec(memory_space=pltpu.SMEM) if x.dtype == jnp.int32 and x.ndim == 1 else VMEM
        for x in operands
    ] + [pl.BlockSpec(memory_space=pl.ANY)] * len(later)
    return pl.pallas_call(
        body_of,
        out_shape=tuple(jax.ShapeDtypeStruct(size, kind) for size, kind in shapes),
        in_specs=in_specs,
        out_specs=(VMEM,) * len(shapes),
        scratch_shapes=scratch,
        compiler_params=pltpu.CompilerParams(vmem_limit_bytes=held_bytes + (room << 20)),
        name=getattr(kernel, "__name__", "step"),
    )(*operands, *later)


def join_parts(ways):
    def join(given_ref, *refs):
        for part, way in enumerate(ways):
            own_ref, came_ref, out_ref = refs[2 * part], refs[2 * part + 1], refs[2 * len(ways) + part]
            for rows, value in joined_rows(given_ref, way, own_ref, came_ref):
                out_ref[rows] = value

    return join


def cond_columns(given_ref, own_ref, came_ref, out_ref, rows_ref):
    for rows, value in joined_rows(given_ref, COND[1], own_ref, came_ref):
        rows_ref[rows] = value
    chip = lax.broadcasted_iota(jnp.int32, (64, 384), 0)
    latent = chip % 32 * 2 + chip // 32
    row = lax.broadcasted_iota(jnp.int32, (64, 384), 1)
    lane = lax.broadcasted_iota(jnp.int32, (128, 128), 0)
    place = lax.broadcasted_iota(jnp.int32, (128, 128), 1)
    total = jnp.zeros((64, 128), F32)
    for tile in range(6):
        values = mm(one_hot(row, 6 * latent + tile), rows_ref[...]).astype(BF)
        wanted = jnp.where(place < 6, given_ref[len(GIVEN)] * 6 + place - 128 * tile, -1)
        total += mm(values, one_hot(lane, wanted))
    out_ref[...] = total.astype(BF)


def split_parts(ways):
    def split(given_ref, *refs):
        count = len(ways)
        for part, way in enumerate(ways):
            value = refs[2 * part][...].astype(F32) + refs[2 * part + 1][...].astype(F32)
            split_rows(
                given_ref, way, value, refs[2 * count + 2 * part], refs[2 * count + 2 * part + 1]
            )

    return split


def split_all(given_ref, *refs):
    keep_ref, send_ref = refs[10], refs[11]
    at = 0
    for part, width in enumerate(BACK_WIDTHS):
        columns = slice(at, at + width)
        value = refs[2 * part][...].astype(F32) + refs[2 * part + 1][...].astype(F32)
        split_rows(given_ref, ("zl", 1, 48), value, keep_ref.at[:, columns], send_ref.at[:, columns])
        at += width


def split_last(given_ref, keep_ref, came_ref, near_keep, near_send, far_keep, far_send):
    value = keep_ref[...] + came_ref[...].astype(F32)
    second = bit_of(given_ref, "x")
    for columns, at in ((slice(0, 1152), 0), (slice(1664, 3200), 1152), (slice(1536, 1664), 2688)):
        first, last = value[:12, columns], value[12:, columns]
        to = slice(at, at + first.shape[1])
        near_keep[:, to] = jnp.where(second, last, first)
        near_send[:, to] = jnp.where(second, first, last)
    first, last = value[:, 3200:3968], value[:, 3968:]
    far_keep[:24] = jnp.where(second, last, first)
    far_send[:24] = jnp.where(second, first, last)
    for half in range(2):
        first, last = [value[12 * half + x : 12 * half + x + 6, 1152:1536] for x in (0, 6)]
        to = slice(384 * half, 384 * half + 384)
        far_keep[24:, to] = jnp.where(second, last, first)
        far_send[24:, to] = jnp.where(second, first, last)


def split_cores(given_ref, keep_ref, came_ref, far_ref, far_came_ref, near_keep, near_send, down_ref, proj_ref):
    value = keep_ref[...] + came_ref[...]
    second = bit_of(given_ref, "c")
    near_keep[...] = jnp.where(second, value[6:], value[:6])
    near_send[...] = jnp.where(second, value[:6], value[6:])
    far = far_ref[...] + far_came_ref[...]
    down_ref[...] = far[:24]
    proj_ref[...] = far[24:]


def ada_grads(core_ref, mod_ref, cond_ref, rows_ref, keep_ref, send_ref, term_ref, sums_ref):
    mods = mod_ref[...].astype(F32)
    mods = jnp.concatenate([mods[:, row, :] for row in range(18)], axis=1).astype(BF)
    pair = mm_tn(cond_ref[...], mods)
    second = bit_of(core_ref, "c")
    keep_ref[...] = jnp.where(second, pair[6:], pair[:6])
    send_ref[...] = jnp.where(second, pair[:6], pair[6:])
    term_ref[...] = mm_nt(mods, rows_ref[...])
    sums_ref[...] = column_sum(mods.astype(F32))


def one_hot(index, at):
    return (index == at).astype(F32).astype(BF)


def row_picks():
    row = lax.broadcasted_iota(jnp.int32, (768, 128), 0)
    device = lax.broadcasted_iota(jnp.int32, (768, 128), 1)
    return one_hot(row, 6 * device)


def bias_vector(units, table_ref):
    rows = mm_tn(row_picks(), units).astype(BF)
    index = lax.broadcasted_iota(jnp.int32, (128, 3840), 0)
    picked = mm_tn(rows, one_hot(index, table_ref[0:1]))
    return column_sum(jnp.where(index == table_ref[1:2], picked, 0.0))


def bias_units(vector, table_ref):
    index = lax.broadcasted_iota(jnp.int32, (128, 3840), 0)
    spread_out = jnp.where(index == table_ref[0:1], vector, 0.0).astype(BF)
    rows = mm_nt(spread_out, one_hot(index, table_ref[1:2])).astype(BF)
    return mm(row_picks(), rows)


def copy_of(value_ref, out_ref):
    out_ref[...] = value_ref[...]


def mod_add(keep_ref, came_ref, out_ref):
    total = keep_ref[...] + came_ref[...]
    for row in range(18):
        out_ref[:, row, :] = total[:, 128 * row : 128 * row + 128]


def mod_sum(got_ref, out_ref):
    total = jnp.sum(got_ref[...], axis=0)
    for row in range(18):
        at = 128 * (row % 6)
        out_ref[row // 6 : row // 6 + 1, at : at + 128] = total[row : row + 1]


def mod_grads(core_ref, start_ref, middle_ref, out_ref, keep_ref, send_ref):
    first = jnp.concatenate([start_ref[...], middle_ref[0:1]], axis=0)
    last = jnp.concatenate([middle_ref[1:3], out_ref[0:1]], axis=0)
    second = core_ref[0] == 1
    keep_ref[...] = jnp.where(second, last, first)
    send_ref[...] = jnp.where(second, first, last)


def mod_join(keep_ref, came_ref, out_ref):
    total = keep_ref[...] + came_ref[...]
    rows = [
        total[row // 6 : row // 6 + 1, 128 * (row % 6) : 128 * (row % 6) + 128] for row in range(18)
    ]
    out_ref[...] = jnp.broadcast_to(jnp.concatenate(rows, axis=0)[None], (64, 18, 128)).astype(BF)


def owners(core_ref, keep_ref, came_ref, qkv_ref, qv_ref, proj_ref, up_ref, up_bias_ref, down_ref):
    keep, came = keep_ref[...], came_ref[...]
    second = core_ref[0] == 1
    left, right = jnp.where(second, came, keep), jnp.where(second, keep, came)
    for part in range(3):
        from_ = slice(384 * part, 384 * part + 384)
        for row in range(6):
            qkv_ref[row, :, 768 * part : 768 * part + 384] = left[row : row + 1, from_]
            qkv_ref[row, :, 768 * part + 384 : 768 * part + 768] = right[row : row + 1, from_]
    for row in range(6):
        up_ref[row, :, :1536] = left[row : row + 1, 1152:2688]
        up_ref[row, :, 1536:] = right[row : row + 1, 1152:2688]
    sums = (keep + came)[0:1, 2688:]
    qv_ref[...] = sums[:, :12]
    up_bias_ref[...] = sums[:, 12:36]
    proj_ref[...] = sums[:, 36:42]
    down_ref[...] = sums[:, 42:48]


def part_ways(core_ref, value, keep_ref, send_ref):
    second = core_ref[0] == 1
    keep_ref[...] = jnp.where(second, value[128:], value[:128])
    send_ref[...] = jnp.where(second, value[:128], value[128:])


def modulate(normed, mod_ref, shift):
    return (normed * (1.0 + mod_ref[shift + 1 : shift + 2]) + mod_ref[shift : shift + 1]).astype(BF)


def column_sum(value):
    return jnp.sum(value, axis=0, keepdims=True)


def first_mix(x_ref, mod_ref, mixed_ref):
    normed, _ = normalize(x_ref[...].astype(F32))
    mixed_ref[...] = modulate(normed, mod_ref, 0)


def attend(
    core_ref, mixed_ref, own_ref, came_ref, bias_table_ref, table_ref,
    bias_ref, weight_ref, qkv_ref, attended_ref, proj_ref, keep_ref, send_ref,
):
    for rows, value in joined_rows(core_ref, OUT[0][2], own_ref, came_ref):
        weight_ref[rows] = value
    bias_ref[...] = bias_vector(weight_ref[:, 1536:], bias_table_ref)
    projected = mm(mixed_ref[...], weight_ref[:, :1152])
    qkv_ref[:, :384] = (projected[:, :384] + bias_ref[:, :384]).astype(BF)
    qkv_ref[:, 384:768] = projected[:, 384:768].astype(BF)
    qkv_ref[:, 768:] = (projected[:, 768:] + bias_ref[:, 384:768]).astype(BF)
    units = weight_ref[:, 1152:1536]
    index = lax.broadcasted_iota(jnp.int32, (384, 768), 1)
    for half in range(2):
        picks = one_hot(index, table_ref[:, half : half + 1])
        proj_ref[:, 384 * half : 384 * half + 384] = mm(picks, units).astype(BF)
    for head in range(6):
        query, keys, values = head_cuts(qkv_ref, head)
        probs = soft_probs(query, keys).astype(BF)
        at = head * HEAD_DIM
        attended_ref[:, at : at + HEAD_DIM] = mm(probs, values).astype(BF)
    part_ways(core_ref, mm(attended_ref[...], proj_ref[...]), keep_ref, send_ref)


def second_mix(keep_ref, came_ref, bias_ref, x_ref, mod_ref, branch_ref, middle_ref, mixed_ref):
    branch = keep_ref[...] + came_ref[...] + bias_ref[:, 2304:3072]
    middle = x_ref[...].astype(F32) + mod_ref[2:3] * branch
    normed, _ = normalize(middle)
    branch_ref[...] = branch
    middle_ref[...] = middle
    mixed_ref[...] = modulate(normed, mod_ref, 3)


def down_rows(pair, half):
    return [(2 * pair + side) * 96 + half * 48 for side in range(2)]


def feed(
    core_ref, mixed_ref, grad_ref, bias_ref, up_own_ref, up_came_ref, own_ref, came_ref,
    keep_ref, send_ref, back_keep_ref, back_send_ref,
    a_keep_ref, a_send_ref, b_keep_ref, b_send_ref, c_keep_ref, c_send_ref, sums_ref,
    hidden_ref, slope_ref, down_ref, up_ref, units_ref,
):
    for rows, value in joined_rows(core_ref, OUT[1][2], up_own_ref, up_came_ref):
        up_ref[rows] = value
    for rows, value in joined_rows(core_ref, OUT[2][2], own_ref, came_ref):
        units_ref[rows] = value
    mixed, grad = mixed_ref[...], grad_ref[...]
    for at in range(0, 1536, 512):
        pre = mm(mixed, up_ref[:, at : at + 512]) + bias_ref[:, 768 + at : 1280 + at]
        square = pre * pre
        tanh = jnp.tanh(0.7978845608028654 * pre * (1.0 + 0.044715 * square))
        half = 0.5 * (1.0 + tanh)
        hidden_ref[:, at : at + 512] = (pre * half).astype(BF)
        slope_ref[:, at : at + 512] = half + 0.5 * pre * (1.0 - tanh * tanh) * (
            0.7978845608028654 * (1.0 + 3.0 * 0.044715 * square)
        )
    for pair in range(8):
        for half in range(2):
            columns = slice(half * 768, half * 768 + 768)
            near = units_ref[48 * pair : 48 * pair + 48, columns].astype(F32)
            far = units_ref[384 + 48 * pair : 432 + 48 * pair, columns].astype(F32)
            for side, row in enumerate(down_rows(pair, half)):
                cut_ = slice(24 * side, 24 * side + 24)
                down_ref[row : row + 48] = jnp.concatenate([near[cut_], far[cut_]]).astype(BF)
    hidden, down = hidden_ref[...], down_ref[...]
    grad_pre = (mm_nt(grad, down) * slope_ref[...]).astype(BF)
    part_ways(core_ref, mm_nt(grad_pre, up_ref[...]), back_keep_ref, back_send_ref)
    part_ways(core_ref, mm(hidden, down), keep_ref, send_ref)
    grad_up = mm_tn(mixed, grad_pre)
    split_rows(core_ref, BACK[2][0], grad_up[:, :1024], a_keep_ref, a_send_ref)
    grad_down = mm_tn(hidden, grad)
    for pair in range(8):
        for half in range(2):
            columns = slice(half * 768, half * 768 + 768)
            for side in range(2):
                units_ref[384 * side + 48 * pair : 384 * side + 48 * pair + 48, columns] = jnp.concatenate(
                    [grad_down[r + 24 * side : r + 24 * side + 24] for r in down_rows(pair, half)]
                ).astype(BF)
    left, right = slice(0, 512), slice(512, 1024)
    split_rows(core_ref, BACK[3][0], grad_up[:, 1024:], b_keep_ref.at[:, left], b_send_ref.at[:, left])
    split_rows(core_ref, BACK[3][0], units_ref[:, :512], b_keep_ref.at[:, right], b_send_ref.at[:, right])
    split_rows(core_ref, BACK[4][0], units_ref[:, 512:], c_keep_ref, c_send_ref)
    sums_ref[...] = column_sum(grad_pre.astype(F32))


def finish(keep_ref, came_ref, bias_ref, middle_ref, grad_ref, mod_ref, out_ref, sums_ref):
    branch = keep_ref[...] + came_ref[...] + bias_ref[:, 3072:3840]
    out_ref[...] = (middle_ref[...] + mod_ref[5:6] * branch).astype(BF)
    grad = grad_ref[...].astype(F32)
    sums_ref[0:1] = column_sum(grad * branch)
    sums_ref[1:2] = column_sum((mod_ref[5:6] * grad).astype(BF).astype(F32))


def middle_back(
    keep_ref, came_ref, middle_ref, branch_ref, grad_ref, mod_ref, grad_middle_ref, grad_branch_ref, sums_ref
):
    grad_mixed = keep_ref[...] + came_ref[...]
    normed, recip = normalize(middle_ref[...])
    grad_middle = grad_ref[...].astype(F32) + norm_back(
        grad_mixed * (1.0 + mod_ref[4:5]), normed, recip
    )
    grad_branch = (mod_ref[2:3] * grad_middle).astype(BF)
    grad_middle_ref[...] = grad_middle
    grad_branch_ref[...] = grad_branch
    sums_ref[0:1] = column_sum(grad_middle * branch_ref[...])
    sums_ref[1:2] = column_sum(grad_mixed)
    sums_ref[2:3] = column_sum(grad_mixed * normed)
    sums_ref[3:4] = column_sum(grad_branch.astype(F32))


def attend_back(
    core_ref, grad_ref, proj_ref, qkv_ref, attended_ref, mixed_ref, weight_ref,
    table_ref, bias_table_ref, up_sums_ref, middle_sums_ref, out_sums_ref,
    keep_ref, send_ref, one_keep_ref, one_send_ref, two_keep_ref, two_send_ref, grad_qkv_ref,
):
    grad = grad_ref[...]
    grad_attended = mm_nt(grad, proj_ref[...]).astype(BF)
    for head in range(6):
        query, keys, values = head_cuts(qkv_ref, head)
        at = head * HEAD_DIM
        grad_out = grad_attended[:, at : at + HEAD_DIM]
        probs = soft_probs(query, keys)
        grad_probs = mm_nt(grad_out, values)
        total = jnp.sum(probs * grad_probs, axis=-1, keepdims=True)
        grad_scores = (probs * (grad_probs - total)).astype(BF)
        grad_qkv_ref[:, at : at + HEAD_DIM] = (mm(grad_scores, keys) * 0.125).astype(BF)
        at += 384
        grad_qkv_ref[:, at : at + HEAD_DIM] = (mm_tn(grad_scores, query) * 0.125).astype(BF)
        at += 384
        grad_qkv_ref[:, at : at + HEAD_DIM] = mm_tn(probs.astype(BF), grad_out).astype(BF)
    grad_qkv = grad_qkv_ref[...]
    part_ways(core_ref, mm_nt(grad_qkv, weight_ref[:, :1152]), keep_ref, send_ref)
    one = mm_tn(mixed_ref[...], grad_qkv[:, :768])
    split_rows(core_ref, BACK[0][0], one, one_keep_ref, one_send_ref)
    grad_proj = mm_tn(attended_ref[...], grad).astype(BF)
    index = lax.broadcasted_iota(jnp.int32, (384, 768), 1)
    units = jnp.zeros((768, 384), F32)
    for half in range(2):
        picks = one_hot(index, table_ref[:, half : half + 1])
        units += mm_tn(picks, grad_proj[:, 384 * half : 384 * half + 384])
    sums = column_sum(grad_qkv.astype(F32))
    vector = jnp.concatenate(
        [sums[:, :384], sums[:, 768:], up_sums_ref[...], middle_sums_ref[3:4], out_sums_ref[1:2]], axis=1
    )
    two = jnp.concatenate(
        [mm_tn(mixed_ref[...], grad_qkv[:, 768:]), units, bias_units(vector, bias_table_ref)], axis=1
    )
    split_rows(core_ref, BACK[1][0], two, two_keep_ref, two_send_ref)


def start_back(keep_ref, came_ref, x_ref, grad_middle_ref, mod_ref, grad_ref, sums_ref):
    grad_mixed = keep_ref[...] + came_ref[...]
    normed, recip = normalize(x_ref[...].astype(F32))
    grad_ref[...] = grad_middle_ref[...] + norm_back(
        grad_mixed * (1.0 + mod_ref[1:2]), normed, recip
    )
    sums_ref[0:1] = column_sum(grad_mixed)
    sums_ref[1:2] = column_sum(grad_mixed * normed)


def body(
    latents_in,
    condition,
    ada_weight,
    ada_bias,
    qkv_weight,
    qv_bias,
    proj_weight,
    proj_bias,
    fc1_weight,
    fc1_bias,
    fc2_weight,
    fc2_bias,
    cotangent,
):
    core = lax.axis_index("c")
    at_s = lax.axis_index("s")
    cond = condition.astype(F32)
    cond_low = jax.nn.silu(cond).astype(BF)

    qkv_cut = qkv_weight[0].reshape(6, 3, 2, 384)
    bias_row = jnp.concatenate([qv_bias, fc1_bias, proj_bias, fc2_bias], axis=1)
    bias_tile = jnp.pad(bias_row, ((0, 5), (0, 128 - 48)))
    first = jnp.concatenate([qkv_cut[:, :, 0].reshape(6, 1152), fc1_weight[0, :, :1536]], axis=1)
    last = jnp.concatenate([qkv_cut[:, :, 1].reshape(6, 1152), fc1_weight[0, :, 1536:]], axis=1)
    mine, theirs = halves(first, last, "c")
    tiles = jnp.concatenate([bias_tile, cond_low.reshape(6, 128)], axis=1)
    mine = jnp.concatenate([mine, tiles], axis=1)
    theirs = jnp.concatenate([theirs, tiles], axis=1)
    other = swap(theirs, "c")
    second = core == 1
    unit12 = jnp.concatenate(
        [jnp.where(second, other, mine), jnp.where(second, mine, other)], axis=0
    )
    unit24 = pair_up(unit12, "x", 0)
    crossed = cross(jnp.concatenate([fc2_weight[0], proj_weight[0]], axis=0))
    crossed = pair_up(crossed[None], "x", 0)
    proj_unit = crossed[:, 24:].reshape(2, 6, 2, 384).transpose(2, 0, 1, 3).reshape(24, 384)
    unit = jnp.concatenate(
        [unit24[:, :1152], proj_unit, unit24[:, 2688:2816], unit24[:, 1152:2688], crossed[0, :24], crossed[1, :24], unit24[:, 2816:]],
        axis=1,
    )
    near = pair_up(pair_up(unit[None], "yl", 0)[None], "zl", 0).reshape(96, 4864)

    which = jnp.stack([lax.axis_index(a) for a in (*GIVEN, NAMES)]).astype(jnp.int32)

    def step_out(parts, ways, later=()):
        pairs = [x for p, way in zip(parts, ways) for x in (p, swap(p, way[0]))]
        shapes = [((p.shape[0] * 2, p.shape[1]), BF) for p in parts]
        return call(join_parts(ways), shapes, which, *pairs, later=later)

    *parts, conds = step_out(cut(near, (*WIDTHS, 128)), [*(way[0] for way in OUT), COND[0]])
    (cond_cols,) = call(
        cond_columns, [((64, 128), BF)], which, conds, swap(conds, "zh"),
        scratch=[pltpu.VMEM((384, 128), BF)],
    )
    cond_cols = cond_cols[:, :6]
    pair_cond = pair_up(cond_cols, "c", 1)

    device = lax.axis_index(NAMES)
    own_bias = lax.dynamic_update_slice(jnp.zeros((4608,), F32), ada_bias[0].astype(F32), (device * 36,))
    partial = mm(cond_cols, ada_weight[0]) + own_bias
    keep, send = halves(partial[:, :2304], partial[:, 2304:], "c")
    (partial,) = call(mod_add, [((64, 18, 128), F32)], keep, swap(send, "c"))
    mod_parts = exchange(partial, CHIPS)
    parts = step_out(parts, [way[1] for way in OUT])
    (mod_half,) = call(mod_sum, [((3, 768), F32)], mod_parts)
    modulation = lax.all_gather(mod_half, "c", axis=0, tiled=True)

    one_own, up_own, units_own = parts
    one_came, up_came, units_came = [swap(p, way[2][0]) for p, way in zip(parts, OUT)]

    proj_rows = jnp.asarray(proj_table())
    bias_places = lax.dynamic_index_in_dim(jnp.asarray(bias_table()), core, 0, False)
    resid, grad_out = cross(latents_in[0]), cross(cotangent[0])
    own = ((128, 768), F32)
    own_low = ((128, 768), BF)
    (mixed_a,) = call(first_mix, [own_low], resid, modulation)
    mixed_a = lax.all_gather(mixed_a, "c", axis=0, tiled=True)
    own_gbb = (modulation[5:6] * grad_out.astype(F32)).astype(BF)
    grad_branch_b = lax.all_gather(own_gbb, "c", axis=0, tiled=True)
    biases, weight_one, qkv, attended, proj_half, keep, send = call(
        attend,
        [((1, 3840), F32), ((768, 1664), BF), ((256, 1152), BF), ((256, 384), BF), ((384, 768), BF), own, own],
        which, mixed_a, one_own, one_came, bias_places, proj_rows,
        room=10,
        later=(grad_branch_b,),
    )
    branch_a, middle, mixed_b = call(
        second_mix, [own, own, own_low], keep, swap(send, "c"), biases, resid, modulation
    )
    mixed_b = lax.all_gather(mixed_b, "c", axis=0, tiled=True)
    out_keep, out_send, keep, send, *feed_parts, up_sums = call(
        feed,
        [own] * 4 + [((384, 1024), BF)] * 6 + [((1, 1536), F32)],
        which, mixed_b, grad_branch_b, biases, up_own, up_came, units_own, units_came,
        scratch=[
            pltpu.VMEM((256, 1536), BF),
            pltpu.VMEM((256, 1536), F32),
            pltpu.VMEM((1536, 768), BF),
            pltpu.VMEM((768, 1536), BF),
            pltpu.VMEM((768, 1536), BF),
        ],
        room=30,
    )
    grad_middle, own_gba, middle_sums = call(
        middle_back,
        [own, own_low, ((4, 768), F32)],
        keep, swap(send, "c"), middle, branch_a, grad_out, modulation,
    )
    grad_branch_a = lax.all_gather(own_gba, "c", axis=0, tiled=True)
    output, out_sums = call(
        finish,
        [own_low, ((2, 768), F32)],
        out_keep, swap(out_send, "c"), biases, middle, grad_out, modulation,
    )
    def step_back(parts, chosen, step, later=()):
        pairs = [x for (k, v), i in zip(parts, chosen) for x in (k, swap(v, BACK[i][step][0]))]
        rows = 192 // (step + 1)
        shapes = [((rows, BACK_WIDTHS[i]), BF) for i in chosen for _ in range(2)]
        ways = [BACK[i][step + 1] for i in chosen]
        done = call(split_parts(ways), shapes, which, *pairs, later=later)
        return list(zip(done[::2], done[1::2]))

    feed_parts = list(zip(feed_parts[::2], feed_parts[1::2]))
    feed_parts = step_back(feed_parts, (2, 3, 4), 0)
    keep, send, one_keep, one_send, two_keep, two_send = call(
        attend_back,
        [own, own] + [((384, 768), BF)] * 2 + [((384, 896), BF)] * 2,
        which, grad_branch_a, proj_half, qkv, attended, mixed_a, weight_one,
        proj_rows, bias_places, up_sums, middle_sums, out_sums,
        scratch=[pltpu.VMEM((256, 1152), BF)],
        room=20,
    )
    grad_resid, start_sums = call(
        start_back,
        [own, ((2, 768), F32)],
        keep, swap(send, "c"), resid, grad_middle, modulation,
        later=feed_parts[0],
    )

    far_one = [(one_keep, one_send), (two_keep, two_send)]
    far_one = step_back(far_one, (0, 1), 0)
    feed_parts = step_back(feed_parts, (2, 3, 4), 1, (far_one[0][0],))
    far_two = step_back(far_one, (0, 1), 1, (feed_parts[0][0],))

    ada_keep, ada_give = halves(ada_weight[0, :, :2304], ada_weight[0, :, 2304:], "c")
    ada_came = swap(ada_give, "c")
    second = core == 1
    ada_rows = jnp.concatenate(
        [jnp.where(second, ada_came, ada_keep), jnp.where(second, ada_keep, ada_came)], axis=0
    )
    keep, send = call(
        mod_grads, [((3, 768), F32)] * 2, which, start_sums, middle_sums, out_sums
    )
    (grad_mod,) = call(mod_join, [((64, 18, 128), BF)], keep, swap(send, "c"), later=feed_parts[0])
    all_mod = exchange(grad_mod, CHIPS)
    keep, give, term, sums = call(
        ada_grads,
        [((6, 2304), F32)] * 2 + [((64, 12), F32), ((1, 2304), F32)],
        which, all_mod, pair_cond, ada_rows,
    )
    came = swap(give, "c")
    grad_ada = jnp.concatenate(
        [jnp.where(second, came, keep), jnp.where(second, keep, came)], axis=1
    )[None]
    ada_sums = jnp.where(core == at_s, sums, swap(sums, "c"))
    grad_ada_bias = lax.dynamic_slice_in_dim(ada_sums, device % 64 * 36, 36, 1)
    term = term.reshape(2, 32, 12).transpose(1, 0, 2).reshape(32, 24)
    term = exchange(jnp.concatenate([term, term], axis=0), CHIPS)

    pairs = [x for (k, v), way in zip(far_two + feed_parts, BACK) for x in (k, swap(v, way[2][0]))]
    keep, send = call(
        split_all, [((48, 4736), F32), ((48, 4736), BF)], which, *pairs
    )
    latents_grad, output = cross(grad_resid), cross(output)
    keep, send = call(
        split_parts([("yl", 1, 24)]), [((24, 4736), F32), ((24, 4736), BF)], which, keep, swap(send, "zl")
    )
    near_keep, near_send, far_keep, far_send = call(
        split_last,
        [((12, 2816), F32)] * 2 + [((30, 768), F32)] * 2,
        which, keep, swap(send, "yl"),
    )
    keep, send, down, proj = call(
        split_cores,
        [((6, 2816), F32)] * 2 + [((24, 768), F32), ((6, 768), F32)],
        which, near_keep, swap(near_send, "x"), far_keep, swap(far_send, "x"),
    )
    grad_fc2, grad_proj = cross(down)[None], cross(proj)[None]
    grad_qkv, grad_qv, grad_proj_bias, grad_fc1, grad_fc1_bias, grad_fc2_bias = call(
        owners,
        [((6, 1, 2304), F32), ((1, 12), F32), ((1, 6), F32), ((6, 1, 3072), F32), ((1, 24), F32), ((1, 6), F32)],
        which, keep, swap(send, "c"),
    )

    (term,) = call(copy_of, [((64, 24), F32)], term, later=(near_keep,))
    term = term.reshape(64, 2, 12).transpose(1, 0, 2).reshape(2, 768)
    cond_sum = pair_sum(term, "c", 0)
    sigmoid = jax.nn.sigmoid(cond)
    cond_grad = cond_sum * (sigmoid * (1.0 + cond * (1.0 - sigmoid)))

    return (
        output[None],
        latents_grad[None],
        cond_grad,
        grad_ada,
        grad_ada_bias,
        grad_qkv.reshape(1, 6, 2304),
        grad_qv,
        grad_proj,
        grad_proj_bias,
        grad_fc1.reshape(1, 6, 3072),
        grad_fc1_bias,
        grad_fc2,
        grad_fc2_bias,
    )


def solution(mesh):
    finer = Mesh(mesh.devices.reshape(SIZES), NAMES)
    tokens = P(NAMES[1:], "s", None)
    cond = P(NAMES[1:], None)
    matrix = P(None, NAMES, None)
    vector = P(None, NAMES)
    weights = (matrix, vector) * 5
    return jax.shard_map(
        body,
        mesh=finer,
        in_specs=(tokens, cond) + weights + (tokens,),
        out_specs=(tokens, tokens, cond) + weights,
        check_vma=False,
    )
```

```python
import jax
import jax.numpy as jnp
import numpy as np
from jax import lax
from jax.experimental import pallas as pl
from jax.experimental.pallas import tpu as pltpu
from jax.sharding import Mesh
from jax.sharding import PartitionSpec as P

HEAD_DIM = 64
EPSILON = 1e-06
BF = jnp.bfloat16
F32 = jnp.float32
SIZES = (2, 2, 2, 2, 2, 2, 2)
NAMES = ("s", "zh", "zl", "yh", "yl", "x", "c")
CHIPS = NAMES[:6]
GIVEN = ("c", "s", "zh", "yh", "zl", "yl", "x")
WIDTHS = (1664, 1536, 1536)
OUT = (
    (("s", 1, 96), ("zh", 2, 96), ("yh", 8, 48)),
    (("zh", 1, 96), ("yh", 4, 48), ("s", 1, 384)),
    (("yh", 2, 48), ("s", 1, 192), ("zh", 2, 192)),
)
COND = (("yh", 2, 48), ("zh", 1, 192))
BACK = (
    (("yh", 8, 48), ("s", 1, 192), ("zh", 1, 96)),
    (("zh", 2, 192), ("yh", 4, 48), ("s", 1, 96)),
    (("s", 1, 384), ("yh", 4, 48), ("zh", 1, 96)),
    (("zh", 2, 192), ("s", 1, 192), ("yh", 2, 48)),
    (("yh", 8, 48), ("zh", 2, 96), ("s", 1, 96)),
)
BACK_WIDTHS = (768, 896, 1024, 1024, 1024)


def bias_table():
    owners, places = [], []
    for core in range(2):
        owner, place = [], []
        for start, count, size, slot in (
            (core * 384, 384, 12, 0),
            (768 + core * 384, 384, 12, 0),
            (core * 1536, 1536, 24, 12),
            (0, 768, 6, 36),
            (0, 768, 6, 42),
        ):
            at = start + np.arange(count)
            owner.append(at // size)
            place.append(slot + at % size)
        owners.append(np.concatenate(owner))
        places.append(np.concatenate(place))
    return np.stack([np.stack(owners), np.stack(places)], axis=1).astype(np.int32)


def proj_table():
    row = np.arange(384)
    unit = row // 6 % 2 * 384 + row // 24 * 24 + row // 12 % 2 * 6 + row % 6
    return np.stack([unit, unit + 12], axis=1).astype(np.int32)


def swap(value, axis):
    return lax.ppermute(value, axis, [(0, 1), (1, 0)])


def cross(value):
    return lax.ppermute(value, ("s", "c"), [(0, 0), (1, 2), (2, 1), (3, 3)])


def pair_up(value, axis, dim):
    other = swap(value, axis)
    second = lax.axis_index(axis) == 1
    return jnp.concatenate(
        [jnp.where(second, other, value), jnp.where(second, value, other)], axis=dim
    )


def halves(first, last, axis):
    second = lax.axis_index(axis) == 1
    return jnp.where(second, last, first), jnp.where(second, first, last)


def pair_sum(value, axis, dim, send_type=F32):
    first, last = jnp.split(value, 2, axis=dim)
    mine, theirs = halves(first, last, axis)
    return mine + swap(theirs.astype(send_type), axis).astype(F32)


def exchange(value, axes):
    return lax.all_to_all(value, axes, 0, 0, tiled=True)


def cut(values, widths):
    start, parts = 0, []
    for width in widths:
        parts.append(values[..., start : start + width])
        start += width
    return parts


def bit_of(given_ref, axis):
    return given_ref[GIVEN.index(axis)] == 1


def joined_rows(given_ref, way, own_ref, came_ref, columns=slice(None)):
    axis, outer, inner = way
    second = bit_of(given_ref, axis)
    for block in range(outer):
        rows = slice(block * inner, block * inner + inner)
        own, came = own_ref[rows, columns], came_ref[rows, columns]
        yield slice(2 * block * inner, (2 * block + 1) * inner), jnp.where(second, came, own)
        yield slice((2 * block + 1) * inner, (2 * block + 2) * inner), jnp.where(second, own, came)


def split_rows(given_ref, way, value, keep_ref, send_ref):
    axis, outer, inner = way
    second = bit_of(given_ref, axis)
    for block in range(outer):
        first = value[2 * block * inner : (2 * block + 1) * inner]
        last = value[(2 * block + 1) * inner : (2 * block + 2) * inner]
        rows = slice(block * inner, block * inner + inner)
        keep_ref[rows] = jnp.where(second, last, first).astype(keep_ref.dtype)
        send_ref[rows] = jnp.where(second, first, last).astype(send_ref.dtype)


def normalize(values):
    centre = values - jnp.mean(values, axis=-1, keepdims=True)
    recip = lax.rsqrt(jnp.mean(centre * centre, axis=-1, keepdims=True) + EPSILON)
    return centre * recip, recip


def norm_back(grad_norm, normed, recip):
    return recip * (
        grad_norm
        - jnp.mean(grad_norm, axis=-1, keepdims=True)
        - normed * jnp.mean(grad_norm * normed, axis=-1, keepdims=True)
    )


def mm(left, right):
    return jnp.dot(left, right, preferred_element_type=F32)


def mm_nt(left, right):
    return lax.dot_general(left, right, (((1,), (1,)), ((), ())), preferred_element_type=F32)


def mm_tn(left, right):
    return lax.dot_general(left, right, (((0,), (0,)), ((), ())), preferred_element_type=F32)


VMEM = pl.BlockSpec(memory_space=pltpu.VMEM)


def soft_probs(query, keys):
    scores = mm_nt(query, keys) * 0.125
    raised = jnp.exp(scores - jnp.max(scores, axis=-1, keepdims=True))
    return raised / jnp.sum(raised, axis=-1, keepdims=True)


def head_cuts(qkv_ref, head):
    at = head * HEAD_DIM
    return [qkv_ref[:, base + at : base + at + HEAD_DIM] for base in (0, 384, 768)]


def call(kernel, shapes, *operands, scratch=(), later=(), room=4):
    body_of = kernel
    if later:
        count, held = len(operands), len(later)

        def body_of(*refs):
            kernel(*refs[:count], *refs[count + held :])

    arrays = [(x.shape, x.dtype) for x in operands] + list(shapes)
    held_bytes = sum(int(np.prod(size)) * jnp.dtype(kind).itemsize for size, kind in arrays)
    in_specs = [
        pl.BlockSpec(memory_space=pltpu.SMEM) if x.dtype == jnp.int32 and x.ndim == 1 else VMEM
        for x in operands
    ] + [pl.BlockSpec(memory_space=pl.ANY)] * len(later)
    return pl.pallas_call(
        body_of,
        out_shape=tuple(jax.ShapeDtypeStruct(size, kind) for size, kind in shapes),
        in_specs=in_specs,
        out_specs=(VMEM,) * len(shapes),
        scratch_shapes=scratch,
        compiler_params=pltpu.CompilerParams(vmem_limit_bytes=held_bytes + (room << 20)),
        name=getattr(kernel, "__name__", "step"),
    )(*operands, *later)


def join_parts(ways):
    def join(given_ref, *refs):
        for part, way in enumerate(ways):
            own_ref, came_ref, out_ref = refs[2 * part], refs[2 * part + 1], refs[2 * len(ways) + part]
            for rows, value in joined_rows(given_ref, way, own_ref, came_ref):
                out_ref[rows] = value

    return join


def cond_columns(given_ref, own_ref, came_ref, out_ref, rows_ref):
    for rows, value in joined_rows(given_ref, COND[1], own_ref, came_ref):
        rows_ref[rows] = value
    chip = lax.broadcasted_iota(jnp.int32, (64, 384), 0)
    latent = chip % 32 * 2 + chip // 32
    row = lax.broadcasted_iota(jnp.int32, (64, 384), 1)
    lane = lax.broadcasted_iota(jnp.int32, (128, 128), 0)
    place = lax.broadcasted_iota(jnp.int32, (128, 128), 1)
    total = jnp.zeros((64, 128), F32)
    for tile in range(6):
        values = mm(one_hot(row, 6 * latent + tile), rows_ref[...]).astype(BF)
        wanted = jnp.where(place < 6, given_ref[len(GIVEN)] * 6 + place - 128 * tile, -1)
        total += mm(values, one_hot(lane, wanted))
    out_ref[...] = total.astype(BF)


def split_parts(ways):
    def split(given_ref, *refs):
        count = len(ways)
        for part, way in enumerate(ways):
            value = refs[2 * part][...].astype(F32) + refs[2 * part + 1][...].astype(F32)
            split_rows(
                given_ref, way, value, refs[2 * count + 2 * part], refs[2 * count + 2 * part + 1]
            )

    return split


def split_all(given_ref, *refs):
    keep_ref, send_ref = refs[10], refs[11]
    at = 0
    for part, width in enumerate(BACK_WIDTHS):
        columns = slice(at, at + width)
        value = refs[2 * part][...].astype(F32) + refs[2 * part + 1][...].astype(F32)
        split_rows(given_ref, ("zl", 1, 48), value, keep_ref.at[:, columns], send_ref.at[:, columns])
        at += width


def split_last(given_ref, keep_ref, came_ref, near_keep, near_send, far_keep, far_send):
    value = keep_ref[...] + came_ref[...].astype(F32)
    second = bit_of(given_ref, "x")
    for columns, at in ((slice(0, 1152), 0), (slice(1664, 3200), 1152), (slice(1536, 1664), 2688)):
        first, last = value[:12, columns], value[12:, columns]
        to = slice(at, at + first.shape[1])
        near_keep[:, to] = jnp.where(second, last, first)
        near_send[:, to] = jnp.where(second, first, last)
    first, last = value[:, 3200:3968], value[:, 3968:]
    far_keep[:24] = jnp.where(second, last, first)
    far_send[:24] = jnp.where(second, first, last)
    for half in range(2):
        first, last = [value[12 * half + x : 12 * half + x + 6, 1152:1536] for x in (0, 6)]
        to = slice(384 * half, 384 * half + 384)
        far_keep[24:, to] = jnp.where(second, last, first)
        far_send[24:, to] = jnp.where(second, first, last)


def split_cores(given_ref, keep_ref, came_ref, far_ref, far_came_ref, near_keep, near_send, down_ref, proj_ref):
    value = keep_ref[...] + came_ref[...]
    second = bit_of(given_ref, "c")
    near_keep[...] = jnp.where(second, value[6:], value[:6])
    near_send[...] = jnp.where(second, value[:6], value[6:])
    far = far_ref[...] + far_came_ref[...]
    down_ref[...] = far[:24]
    proj_ref[...] = far[24:]


def ada_grads(core_ref, mod_ref, cond_ref, rows_ref, keep_ref, send_ref, term_ref, sums_ref):
    mods = mod_ref[...].astype(F32)
    mods = jnp.concatenate([mods[:, row, :] for row in range(18)], axis=1).astype(BF)
    pair = mm_tn(cond_ref[...], mods)
    second = bit_of(core_ref, "c")
    keep_ref[...] = jnp.where(second, pair[6:], pair[:6])
    send_ref[...] = jnp.where(second, pair[:6], pair[6:])
    term_ref[...] = mm_nt(mods, rows_ref[...])
    sums_ref[...] = column_sum(mods.astype(F32))


def one_hot(index, at):
    return (index == at).astype(F32).astype(BF)


def row_picks():
    row = lax.broadcasted_iota(jnp.int32, (768, 128), 0)
    device = lax.broadcasted_iota(jnp.int32, (768, 128), 1)
    return one_hot(row, 6 * device)


def bias_vector(units, table_ref):
    rows = mm_tn(row_picks(), units).astype(BF)
    index = lax.broadcasted_iota(jnp.int32, (128, 3840), 0)
    picked = mm_tn(rows, one_hot(index, table_ref[0:1]))
    return column_sum(jnp.where(index == table_ref[1:2], picked, 0.0))


def bias_units(vector, table_ref):
    index = lax.broadcasted_iota(jnp.int32, (128, 3840), 0)
    spread_out = jnp.where(index == table_ref[0:1], vector, 0.0).astype(BF)
    rows = mm_nt(spread_out, one_hot(index, table_ref[1:2])).astype(BF)
    return mm(row_picks(), rows)


def copy_of(value_ref, out_ref):
    out_ref[...] = value_ref[...]


def mod_add(keep_ref, came_ref, out_ref):
    total = keep_ref[...] + came_ref[...]
    for row in range(18):
        out_ref[:, row, :] = total[:, 128 * row : 128 * row + 128]


def mod_sum(got_ref, out_ref):
    total = jnp.sum(got_ref[...], axis=0)
    for row in range(18):
        at = 128 * (row % 6)
        out_ref[row // 6 : row // 6 + 1, at : at + 128] = total[row : row + 1]


def mod_grads(core_ref, start_ref, middle_ref, out_ref, keep_ref, send_ref):
    first = jnp.concatenate([start_ref[...], middle_ref[0:1]], axis=0)
    last = jnp.concatenate([middle_ref[1:3], out_ref[0:1]], axis=0)
    second = core_ref[0] == 1
    keep_ref[...] = jnp.where(second, last, first)
    send_ref[...] = jnp.where(second, first, last)


def mod_join(keep_ref, came_ref, out_ref):
    total = keep_ref[...] + came_ref[...]
    rows = [
        total[row // 6 : row // 6 + 1, 128 * (row % 6) : 128 * (row % 6) + 128] for row in range(18)
    ]
    out_ref[...] = jnp.broadcast_to(jnp.concatenate(rows, axis=0)[None], (64, 18, 128)).astype(BF)


def owners(core_ref, keep_ref, came_ref, qkv_ref, qv_ref, proj_ref, up_ref, up_bias_ref, down_ref):
    keep, came = keep_ref[...], came_ref[...]
    second = core_ref[0] == 1
    left, right = jnp.where(second, came, keep), jnp.where(second, keep, came)
    for part in range(3):
        from_ = slice(384 * part, 384 * part + 384)
        for row in range(6):
            qkv_ref[row, :, 768 * part : 768 * part + 384] = left[row : row + 1, from_]
            qkv_ref[row, :, 768 * part + 384 : 768 * part + 768] = right[row : row + 1, from_]
    for row in range(6):
        up_ref[row, :, :1536] = left[row : row + 1, 1152:2688]
        up_ref[row, :, 1536:] = right[row : row + 1, 1152:2688]
    sums = (keep + came)[0:1, 2688:]
    qv_ref[...] = sums[:, :12]
    up_bias_ref[...] = sums[:, 12:36]
    proj_ref[...] = sums[:, 36:42]
    down_ref[...] = sums[:, 42:48]


def part_ways(core_ref, value, keep_ref, send_ref):
    second = core_ref[0] == 1
    keep_ref[...] = jnp.where(second, value[128:], value[:128])
    send_ref[...] = jnp.where(second, value[:128], value[128:])


def modulate(normed, mod_ref, shift):
    return (normed * (1.0 + mod_ref[shift + 1 : shift + 2]) + mod_ref[shift : shift + 1]).astype(BF)


def column_sum(value):
    return jnp.sum(value, axis=0, keepdims=True)


def first_mix(x_ref, mod_ref, mixed_ref):
    normed, _ = normalize(x_ref[...].astype(F32))
    mixed_ref[...] = modulate(normed, mod_ref, 0)


def attend(
    core_ref, mixed_ref, own_ref, came_ref, bias_table_ref, table_ref,
    bias_ref, weight_ref, qkv_ref, attended_ref, proj_ref, keep_ref, send_ref,
):
    for rows, value in joined_rows(core_ref, OUT[0][2], own_ref, came_ref):
        weight_ref[rows] = value
    bias_ref[...] = bias_vector(weight_ref[:, 1536:], bias_table_ref)
    projected = mm(mixed_ref[...], weight_ref[:, :1152])
    qkv_ref[:, :384] = (projected[:, :384] + bias_ref[:, :384]).astype(BF)
    qkv_ref[:, 384:768] = projected[:, 384:768].astype(BF)
    qkv_ref[:, 768:] = (projected[:, 768:] + bias_ref[:, 384:768]).astype(BF)
    units = weight_ref[:, 1152:1536]
    index = lax.broadcasted_iota(jnp.int32, (384, 768), 1)
    for half in range(2):
        picks = one_hot(index, table_ref[:, half : half + 1])
        proj_ref[:, 384 * half : 384 * half + 384] = mm(picks, units).astype(BF)
    for head in range(6):
        query, keys, values = head_cuts(qkv_ref, head)
        probs = soft_probs(query, keys).astype(BF)
        at = head * HEAD_DIM
        attended_ref[:, at : at + HEAD_DIM] = mm(probs, values).astype(BF)
    part_ways(core_ref, mm(attended_ref[...], proj_ref[...]), keep_ref, send_ref)


def second_mix(keep_ref, came_ref, bias_ref, x_ref, mod_ref, branch_ref, middle_ref, mixed_ref):
    branch = keep_ref[...] + came_ref[...] + bias_ref[:, 2304:3072]
    middle = x_ref[...].astype(F32) + mod_ref[2:3] * branch
    normed, _ = normalize(middle)
    branch_ref[...] = branch
    middle_ref[...] = middle
    mixed_ref[...] = modulate(normed, mod_ref, 3)


def down_rows(pair, half):
    return [(2 * pair + side) * 96 + half * 48 for side in range(2)]


def feed(
    core_ref, mixed_ref, grad_ref, bias_ref, up_own_ref, up_came_ref, own_ref, came_ref,
    keep_ref, send_ref, back_keep_ref, back_send_ref,
    a_keep_ref, a_send_ref, b_keep_ref, b_send_ref, c_keep_ref, c_send_ref, sums_ref,
    hidden_ref, slope_ref, down_ref, up_ref, units_ref,
):
    for rows, value in joined_rows(core_ref, OUT[1][2], up_own_ref, up_came_ref):
        up_ref[rows] = value
    for rows, value in joined_rows(core_ref, OUT[2][2], own_ref, came_ref):
        units_ref[rows] = value
    mixed, grad = mixed_ref[...], grad_ref[...]
    for at in range(0, 1536, 512):
        pre = mm(mixed, up_ref[:, at : at + 512]) + bias_ref[:, 768 + at : 1280 + at]
        square = pre * pre
        tanh = jnp.tanh(0.7978845608028654 * pre * (1.0 + 0.044715 * square))
        half = 0.5 * (1.0 + tanh)
        hidden_ref[:, at : at + 512] = (pre * half).astype(BF)
        slope_ref[:, at : at + 512] = half + 0.5 * pre * (1.0 - tanh * tanh) * (
            0.7978845608028654 * (1.0 + 3.0 * 0.044715 * square)
        )
    for pair in range(8):
        for half in range(2):
            columns = slice(half * 768, half * 768 + 768)
            near = units_ref[48 * pair : 48 * pair + 48, columns].astype(F32)
            far = units_ref[384 + 48 * pair : 432 + 48 * pair, columns].astype(F32)
            for side, row in enumerate(down_rows(pair, half)):
                cut_ = slice(24 * side, 24 * side + 24)
                down_ref[row : row + 48] = jnp.concatenate([near[cut_], far[cut_]]).astype(BF)
    hidden, down = hidden_ref[...], down_ref[...]
    grad_pre = (mm_nt(grad, down) * slope_ref[...]).astype(BF)
    part_ways(core_ref, mm_nt(grad_pre, up_ref[...]), back_keep_ref, back_send_ref)
    part_ways(core_ref, mm(hidden, down), keep_ref, send_ref)
    grad_up = mm_tn(mixed, grad_pre)
    split_rows(core_ref, BACK[2][0], grad_up[:, :1024], a_keep_ref, a_send_ref)
    grad_down = mm_tn(hidden, grad)
    for pair in range(8):
        for half in range(2):
            columns = slice(half * 768, half * 768 + 768)
            for side in range(2):
                units_ref[384 * side + 48 * pair : 384 * side + 48 * pair + 48, columns] = jnp.concatenate(
                    [grad_down[r + 24 * side : r + 24 * side + 24] for r in down_rows(pair, half)]
                ).astype(BF)
    left, right = slice(0, 512), slice(512, 1024)
    split_rows(core_ref, BACK[3][0], grad_up[:, 1024:], b_keep_ref.at[:, left], b_send_ref.at[:, left])
    split_rows(core_ref, BACK[3][0], units_ref[:, :512], b_keep_ref.at[:, right], b_send_ref.at[:, right])
    split_rows(core_ref, BACK[4][0], units_ref[:, 512:], c_keep_ref, c_send_ref)
    sums_ref[...] = column_sum(grad_pre.astype(F32))


def finish(keep_ref, came_ref, bias_ref, middle_ref, grad_ref, mod_ref, out_ref, sums_ref):
    branch = keep_ref[...] + came_ref[...] + bias_ref[:, 3072:3840]
    out_ref[...] = (middle_ref[...] + mod_ref[5:6] * branch).astype(BF)
    grad = grad_ref[...].astype(F32)
    sums_ref[0:1] = column_sum(grad * branch)
    sums_ref[1:2] = column_sum((mod_ref[5:6] * grad).astype(BF).astype(F32))


def middle_back(
    keep_ref, came_ref, middle_ref, branch_ref, grad_ref, mod_ref, grad_middle_ref, grad_branch_ref, sums_ref
):
    grad_mixed = keep_ref[...] + came_ref[...]
    normed, recip = normalize(middle_ref[...])
    grad_middle = grad_ref[...].astype(F32) + norm_back(
        grad_mixed * (1.0 + mod_ref[4:5]), normed, recip
    )
    grad_branch = (mod_ref[2:3] * grad_middle).astype(BF)
    grad_middle_ref[...] = grad_middle
    grad_branch_ref[...] = grad_branch
    sums_ref[0:1] = column_sum(grad_middle * branch_ref[...])
    sums_ref[1:2] = column_sum(grad_mixed)
    sums_ref[2:3] = column_sum(grad_mixed * normed)
    sums_ref[3:4] = column_sum(grad_branch.astype(F32))


def attend_back(
    core_ref, grad_ref, proj_ref, qkv_ref, attended_ref, mixed_ref, weight_ref,
    table_ref, bias_table_ref, up_sums_ref, middle_sums_ref, out_sums_ref,
    keep_ref, send_ref, one_keep_ref, one_send_ref, two_keep_ref, two_send_ref, grad_qkv_ref,
):
    grad = grad_ref[...]
    grad_attended = mm_nt(grad, proj_ref[...]).astype(BF)
    for head in range(6):
        query, keys, values = head_cuts(qkv_ref, head)
        at = head * HEAD_DIM
        grad_out = grad_attended[:, at : at + HEAD_DIM]
        probs = soft_probs(query, keys)
        grad_probs = mm_nt(grad_out, values)
        total = jnp.sum(probs * grad_probs, axis=-1, keepdims=True)
        grad_scores = (probs * (grad_probs - total)).astype(BF)
        grad_qkv_ref[:, at : at + HEAD_DIM] = (mm(grad_scores, keys) * 0.125).astype(BF)
        at += 384
        grad_qkv_ref[:, at : at + HEAD_DIM] = (mm_tn(grad_scores, query) * 0.125).astype(BF)
        at += 384
        grad_qkv_ref[:, at : at + HEAD_DIM] = mm_tn(probs.astype(BF), grad_out).astype(BF)
    grad_qkv = grad_qkv_ref[...]
    part_ways(core_ref, mm_nt(grad_qkv, weight_ref[:, :1152]), keep_ref, send_ref)
    one = mm_tn(mixed_ref[...], grad_qkv[:, :768])
    split_rows(core_ref, BACK[0][0], one, one_keep_ref, one_send_ref)
    grad_proj = mm_tn(attended_ref[...], grad).astype(BF)
    index = lax.broadcasted_iota(jnp.int32, (384, 768), 1)
    units = jnp.zeros((768, 384), F32)
    for half in range(2):
        picks = one_hot(index, table_ref[:, half : half + 1])
        units += mm_tn(picks, grad_proj[:, 384 * half : 384 * half + 384])
    sums = column_sum(grad_qkv.astype(F32))
    vector = jnp.concatenate(
        [sums[:, :384], sums[:, 768:], up_sums_ref[...], middle_sums_ref[3:4], out_sums_ref[1:2]], axis=1
    )
    two = jnp.concatenate(
        [mm_tn(mixed_ref[...], grad_qkv[:, 768:]), units, bias_units(vector, bias_table_ref)], axis=1
    )
    split_rows(core_ref, BACK[1][0], two, two_keep_ref, two_send_ref)


def start_back(keep_ref, came_ref, x_ref, grad_middle_ref, mod_ref, grad_ref, sums_ref):
    grad_mixed = keep_ref[...] + came_ref[...]
    normed, recip = normalize(x_ref[...].astype(F32))
    grad_ref[...] = grad_middle_ref[...] + norm_back(
        grad_mixed * (1.0 + mod_ref[1:2]), normed, recip
    )
    sums_ref[0:1] = column_sum(grad_mixed)
    sums_ref[1:2] = column_sum(grad_mixed * normed)


def body(
    latents_in,
    condition,
    ada_weight,
    ada_bias,
    qkv_weight,
    qv_bias,
    proj_weight,
    proj_bias,
    fc1_weight,
    fc1_bias,
    fc2_weight,
    fc2_bias,
    cotangent,
):
    core = lax.axis_index("c")
    at_s = lax.axis_index("s")
    cond = condition.astype(F32)
    cond_low = jax.nn.silu(cond).astype(BF)

    qkv_cut = qkv_weight[0].reshape(6, 3, 2, 384)
    bias_row = jnp.concatenate([qv_bias, fc1_bias, proj_bias, fc2_bias], axis=1)
    bias_tile = jnp.pad(bias_row, ((0, 5), (0, 128 - 48)))
    first = jnp.concatenate([qkv_cut[:, :, 0].reshape(6, 1152), fc1_weight[0, :, :1536]], axis=1)
    last = jnp.concatenate([qkv_cut[:, :, 1].reshape(6, 1152), fc1_weight[0, :, 1536:]], axis=1)
    mine, theirs = halves(first, last, "c")
    tiles = jnp.concatenate([bias_tile, cond_low.reshape(6, 128)], axis=1)
    mine = jnp.concatenate([mine, tiles], axis=1)
    theirs = jnp.concatenate([theirs, tiles], axis=1)
    other = swap(theirs, "c")
    second = core == 1
    unit12 = jnp.concatenate(
        [jnp.where(second, other, mine), jnp.where(second, mine, other)], axis=0
    )
    unit24 = pair_up(unit12, "x", 0)
    crossed = cross(jnp.concatenate([fc2_weight[0], proj_weight[0]], axis=0))
    crossed = pair_up(crossed[None], "x", 0)
    proj_unit = crossed[:, 24:].reshape(2, 6, 2, 384).transpose(2, 0, 1, 3).reshape(24, 384)
    unit = jnp.concatenate(
        [unit24[:, :1152], proj_unit, unit24[:, 2688:2816], unit24[:, 1152:2688], crossed[0, :24], crossed[1, :24], unit24[:, 2816:]],
        axis=1,
    )
    near = pair_up(pair_up(unit[None], "yl", 0)[None], "zl", 0).reshape(96, 4864)

    which = jnp.stack([lax.axis_index(a) for a in (*GIVEN, NAMES)]).astype(jnp.int32)

    def step_out(parts, ways, later=()):
        pairs = [x for p, way in zip(parts, ways) for x in (p, swap(p, way[0]))]
        shapes = [((p.shape[0] * 2, p.shape[1]), BF) for p in parts]
        return call(join_parts(ways), shapes, which, *pairs, later=later)

    *parts, conds = step_out(cut(near, (*WIDTHS, 128)), [*(way[0] for way in OUT), COND[0]])
    (cond_cols,) = call(
        cond_columns, [((64, 128), BF)], which, conds, swap(conds, "zh"),
        scratch=[pltpu.VMEM((384, 128), BF)],
    )
    cond_cols = cond_cols[:, :6]
    pair_cond = pair_up(cond_cols, "c", 1)

    device = lax.axis_index(NAMES)
    own_bias = lax.dynamic_update_slice(jnp.zeros((4608,), F32), ada_bias[0].astype(F32), (device * 36,))
    partial = mm(cond_cols, ada_weight[0]) + own_bias
    keep, send = halves(partial[:, :2304], partial[:, 2304:], "c")
    (partial,) = call(mod_add, [((64, 18, 128), F32)], keep, swap(send, "c"))
    mod_parts = exchange(partial, CHIPS)
    one = step_out(parts[:1], [OUT[0][1]])
    parts = [*one, *step_out(parts[1:], [way[1] for way in OUT[1:]], (mod_parts,))]
    (mod_half,) = call(mod_sum, [((3, 768), F32)], mod_parts)
    modulation = lax.all_gather(mod_half, "c", axis=0, tiled=True)

    one_own, up_own, units_own = parts
    one_came, up_came, units_came = [swap(p, way[2][0]) for p, way in zip(parts, OUT)]

    proj_rows = jnp.asarray(proj_table())
    bias_places = lax.dynamic_index_in_dim(jnp.asarray(bias_table()), core, 0, False)
    resid, grad_out = cross(latents_in[0]), cross(cotangent[0])
    own = ((128, 768), F32)
    own_low = ((128, 768), BF)
    (mixed_a,) = call(first_mix, [own_low], resid, modulation)
    mixed_a = lax.all_gather(mixed_a, "c", axis=0, tiled=True)
    own_gbb = (modulation[5:6] * grad_out.astype(F32)).astype(BF)
    grad_branch_b = lax.all_gather(own_gbb, "c", axis=0, tiled=True)
    biases, weight_one, qkv, attended, proj_half, keep, send = call(
        attend,
        [((1, 3840), F32), ((768, 1664), BF), ((256, 1152), BF), ((256, 384), BF), ((384, 768), BF), own, own],
        which, mixed_a, one_own, one_came, bias_places, proj_rows,
        room=10,
        later=(grad_branch_b,),
    )
    branch_a, middle, mixed_b = call(
        second_mix, [own, own, own_low], keep, swap(send, "c"), biases, resid, modulation
    )
    mixed_b = lax.all_gather(mixed_b, "c", axis=0, tiled=True)
    out_keep, out_send, keep, send, *feed_parts, up_sums = call(
        feed,
        [own] * 4 + [((384, 1024), BF)] * 6 + [((1, 1536), F32)],
        which, mixed_b, grad_branch_b, biases, up_own, up_came, units_own, units_came,
        scratch=[
            pltpu.VMEM((256, 1536), BF),
            pltpu.VMEM((256, 1536), F32),
            pltpu.VMEM((1536, 768), BF),
            pltpu.VMEM((768, 1536), BF),
            pltpu.VMEM((768, 1536), BF),
        ],
        room=30,
    )
    grad_middle, own_gba, middle_sums = call(
        middle_back,
        [own, own_low, ((4, 768), F32)],
        keep, swap(send, "c"), middle, branch_a, grad_out, modulation,
    )
    grad_branch_a = lax.all_gather(own_gba, "c", axis=0, tiled=True)
    output, out_sums = call(
        finish,
        [own_low, ((2, 768), F32)],
        out_keep, swap(out_send, "c"), biases, middle, grad_out, modulation,
    )
    def step_back(parts, chosen, step, later=()):
        pairs = [x for (k, v), i in zip(parts, chosen) for x in (k, swap(v, BACK[i][step][0]))]
        rows = 192 // (step + 1)
        shapes = [((rows, BACK_WIDTHS[i]), BF) for i in chosen for _ in range(2)]
        ways = [BACK[i][step + 1] for i in chosen]
        done = call(split_parts(ways), shapes, which, *pairs, later=later)
        return list(zip(done[::2], done[1::2]))

    feed_parts = list(zip(feed_parts[::2], feed_parts[1::2]))
    feed_parts = step_back(feed_parts, (2, 3, 4), 0)
    keep, send, one_keep, one_send, two_keep, two_send = call(
        attend_back,
        [own, own] + [((384, 768), BF)] * 2 + [((384, 896), BF)] * 2,
        which, grad_branch_a, proj_half, qkv, attended, mixed_a, weight_one,
        proj_rows, bias_places, up_sums, middle_sums, out_sums,
        scratch=[pltpu.VMEM((256, 1152), BF)],
        room=20,
    )
    grad_resid, start_sums = call(
        start_back,
        [own, ((2, 768), F32)],
        keep, swap(send, "c"), resid, grad_middle, modulation,
        later=feed_parts[0],
    )

    far_one = [(one_keep, one_send), (two_keep, two_send)]
    far_one = step_back(far_one, (0, 1), 0)
    feed_parts = step_back(feed_parts, (2, 3, 4), 1, (far_one[0][0],))
    far_two = step_back(far_one, (0, 1), 1, (feed_parts[0][0],))

    ada_keep, ada_give = halves(ada_weight[0, :, :2304], ada_weight[0, :, 2304:], "c")
    ada_came = swap(ada_give, "c")
    second = core == 1
    ada_rows = jnp.concatenate(
        [jnp.where(second, ada_came, ada_keep), jnp.where(second, ada_keep, ada_came)], axis=0
    )
    keep, send = call(
        mod_grads, [((3, 768), F32)] * 2, which, start_sums, middle_sums, out_sums
    )
    (grad_mod,) = call(mod_join, [((64, 18, 128), BF)], keep, swap(send, "c"), later=feed_parts[0])
    all_mod = exchange(grad_mod, CHIPS)
    keep, give, term, sums = call(
        ada_grads,
        [((6, 2304), F32)] * 2 + [((64, 12), F32), ((1, 2304), F32)],
        which, all_mod, pair_cond, ada_rows,
    )
    came = swap(give, "c")
    grad_ada = jnp.concatenate(
        [jnp.where(second, came, keep), jnp.where(second, keep, came)], axis=1
    )[None]
    ada_sums = jnp.where(core == at_s, sums, swap(sums, "c"))
    grad_ada_bias = lax.dynamic_slice_in_dim(ada_sums, device % 64 * 36, 36, 1)
    term = term.reshape(2, 32, 12).transpose(1, 0, 2).reshape(32, 24)
    term = exchange(jnp.concatenate([term, term], axis=0), CHIPS)

    pairs = [x for (k, v), way in zip(far_two + feed_parts, BACK) for x in (k, swap(v, way[2][0]))]
    keep, send = call(
        split_all, [((48, 4736), F32), ((48, 4736), BF)], which, *pairs
    )
    latents_grad, output = cross(grad_resid), cross(output)
    keep, send = call(
        split_parts([("yl", 1, 24)]), [((24, 4736), F32), ((24, 4736), BF)], which, keep, swap(send, "zl")
    )
    near_keep, near_send, far_keep, far_send = call(
        split_last,
        [((12, 2816), F32)] * 2 + [((30, 768), F32)] * 2,
        which, keep, swap(send, "yl"),
    )
    keep, send, down, proj = call(
        split_cores,
        [((6, 2816), F32)] * 2 + [((24, 768), F32), ((6, 768), F32)],
        which, near_keep, swap(near_send, "x"), far_keep, swap(far_send, "x"),
    )
    grad_fc2, grad_proj = cross(down)[None], cross(proj)[None]
    grad_qkv, grad_qv, grad_proj_bias, grad_fc1, grad_fc1_bias, grad_fc2_bias = call(
        owners,
        [((6, 1, 2304), F32), ((1, 12), F32), ((1, 6), F32), ((6, 1, 3072), F32), ((1, 24), F32), ((1, 6), F32)],
        which, keep, swap(send, "c"),
    )

    (term,) = call(copy_of, [((64, 24), F32)], term, later=(near_keep,))
    term = term.reshape(64, 2, 12).transpose(1, 0, 2).reshape(2, 768)
    cond_sum = pair_sum(term, "c", 0)
    sigmoid = jax.nn.sigmoid(cond)
    cond_grad = cond_sum * (sigmoid * (1.0 + cond * (1.0 - sigmoid)))

    return (
        output[None],
        latents_grad[None],
        cond_grad,
        grad_ada,
        grad_ada_bias,
        grad_qkv.reshape(1, 6, 2304),
        grad_qv,
        grad_proj,
        grad_proj_bias,
        grad_fc1.reshape(1, 6, 3072),
        grad_fc1_bias,
        grad_fc2,
        grad_fc2_bias,
    )


def solution(mesh):
    finer = Mesh(mesh.devices.reshape(SIZES), NAMES)
    tokens = P(NAMES[1:], "s", None)
    cond = P(NAMES[1:], None)
    matrix = P(None, NAMES, None)
    vector = P(None, NAMES)
    weights = (matrix, vector) * 5
    return jax.shard_map(
        body,
        mesh=finer,
        in_specs=(tokens, cond) + weights + (tokens,),
        out_specs=(tokens, tokens, cond) + weights,
        check_vma=False,
    )
```

```python
import jax
import jax.numpy as jnp
import numpy as np
from jax import lax
from jax.experimental import pallas as pl
from jax.experimental.pallas import tpu as pltpu
from jax.sharding import Mesh
from jax.sharding import PartitionSpec as P

HEAD_DIM = 64
EPSILON = 1e-06
BF = jnp.bfloat16
F32 = jnp.float32
SIZES = (2, 2, 2, 2, 2, 2, 2)
NAMES = ("s", "zh", "zl", "yh", "yl", "x", "c")
CHIPS = NAMES[:6]
GIVEN = ("c", "s", "zh", "yh", "zl", "yl", "x")
WIDTHS = (1664, 1536, 1536)
OUT = (
    (("s", 1, 96), ("zh", 2, 96), ("yh", 8, 48)),
    (("zh", 1, 96), ("yh", 4, 48), ("s", 1, 384)),
    (("yh", 2, 48), ("s", 1, 192), ("zh", 2, 192)),
)
COND = (("yh", 2, 48), ("zh", 1, 192))
BACK = (
    (("yh", 8, 48), ("s", 1, 192), ("zh", 1, 96)),
    (("zh", 2, 192), ("yh", 4, 48), ("s", 1, 96)),
    (("s", 1, 384), ("yh", 4, 48), ("zh", 1, 96)),
    (("zh", 2, 192), ("s", 1, 192), ("yh", 2, 48)),
    (("yh", 8, 48), ("zh", 2, 96), ("s", 1, 96)),
)
BACK_WIDTHS = (768, 896, 1024, 1024, 1024)


def bias_table():
    owners, places = [], []
    for core in range(2):
        owner, place = [], []
        for start, count, size, slot in (
            (core * 384, 384, 12, 0),
            (768 + core * 384, 384, 12, 0),
            (core * 1536, 1536, 24, 12),
            (0, 768, 6, 36),
            (0, 768, 6, 42),
        ):
            at = start + np.arange(count)
            owner.append(at // size)
            place.append(slot + at % size)
        owners.append(np.concatenate(owner))
        places.append(np.concatenate(place))
    return np.stack([np.stack(owners), np.stack(places)], axis=1).astype(np.int32)


def proj_table():
    row = np.arange(384)
    unit = row // 6 % 2 * 384 + row // 24 * 24 + row // 12 % 2 * 6 + row % 6
    return np.stack([unit, unit + 12], axis=1).astype(np.int32)


def swap(value, axis):
    return lax.ppermute(value, axis, [(0, 1), (1, 0)])


def cross(value):
    return lax.ppermute(value, ("s", "c"), [(0, 0), (1, 2), (2, 1), (3, 3)])


def pair_up(value, axis, dim):
    other = swap(value, axis)
    second = lax.axis_index(axis) == 1
    return jnp.concatenate(
        [jnp.where(second, other, value), jnp.where(second, value, other)], axis=dim
    )


def halves(first, last, axis):
    second = lax.axis_index(axis) == 1
    return jnp.where(second, last, first), jnp.where(second, first, last)


def pair_sum(value, axis, dim, send_type=F32):
    first, last = jnp.split(value, 2, axis=dim)
    mine, theirs = halves(first, last, axis)
    return mine + swap(theirs.astype(send_type), axis).astype(F32)


def exchange(value, axes):
    return lax.all_to_all(value, axes, 0, 0, tiled=True)


def cut(values, widths):
    start, parts = 0, []
    for width in widths:
        parts.append(values[..., start : start + width])
        start += width
    return parts


def bit_of(given_ref, axis):
    return given_ref[GIVEN.index(axis)] == 1


def joined_rows(given_ref, way, own_ref, came_ref, columns=slice(None)):
    axis, outer, inner = way
    second = bit_of(given_ref, axis)
    for block in range(outer):
        rows = slice(block * inner, block * inner + inner)
        own, came = own_ref[rows, columns], came_ref[rows, columns]
        yield slice(2 * block * inner, (2 * block + 1) * inner), jnp.where(second, came, own)
        yield slice((2 * block + 1) * inner, (2 * block + 2) * inner), jnp.where(second, own, came)


def split_rows(given_ref, way, value, keep_ref, send_ref):
    axis, outer, inner = way
    second = bit_of(given_ref, axis)
    for block in range(outer):
        first = value[2 * block * inner : (2 * block + 1) * inner]
        last = value[(2 * block + 1) * inner : (2 * block + 2) * inner]
        rows = slice(block * inner, block * inner + inner)
        keep_ref[rows] = jnp.where(second, last, first).astype(keep_ref.dtype)
        send_ref[rows] = jnp.where(second, first, last).astype(send_ref.dtype)


def normalize(values):
    centre = values - jnp.mean(values, axis=-1, keepdims=True)
    recip = lax.rsqrt(jnp.mean(centre * centre, axis=-1, keepdims=True) + EPSILON)
    return centre * recip, recip


def norm_back(grad_norm, normed, recip):
    return recip * (
        grad_norm
        - jnp.mean(grad_norm, axis=-1, keepdims=True)
        - normed * jnp.mean(grad_norm * normed, axis=-1, keepdims=True)
    )


def mm(left, right):
    return jnp.dot(left, right, preferred_element_type=F32)


def mm_nt(left, right):
    return lax.dot_general(left, right, (((1,), (1,)), ((), ())), preferred_element_type=F32)


def mm_tn(left, right):
    return lax.dot_general(left, right, (((0,), (0,)), ((), ())), preferred_element_type=F32)


VMEM = pl.BlockSpec(memory_space=pltpu.VMEM)


def soft_probs(query, keys):
    scores = mm_nt(query, keys) * 0.125
    raised = jnp.exp(scores - jnp.max(scores, axis=-1, keepdims=True))
    return raised / jnp.sum(raised, axis=-1, keepdims=True)


def head_cuts(qkv_ref, head):
    at = head * HEAD_DIM
    return [qkv_ref[:, base + at : base + at + HEAD_DIM] for base in (0, 384, 768)]


def call(kernel, shapes, *operands, scratch=(), later=(), room=4):
    body_of = kernel
    if later:
        count, held = len(operands), len(later)

        def body_of(*refs):
            kernel(*refs[:count], *refs[count + held :])

    arrays = [(x.shape, x.dtype) for x in operands] + list(shapes)
    held_bytes = sum(int(np.prod(size)) * jnp.dtype(kind).itemsize for size, kind in arrays)
    in_specs = [
        pl.BlockSpec(memory_space=pltpu.SMEM) if x.dtype == jnp.int32 and x.ndim == 1 else VMEM
        for x in operands
    ] + [pl.BlockSpec(memory_space=pl.ANY)] * len(later)
    return pl.pallas_call(
        body_of,
        out_shape=tuple(jax.ShapeDtypeStruct(size, kind) for size, kind in shapes),
        in_specs=in_specs,
        out_specs=(VMEM,) * len(shapes),
        scratch_shapes=scratch,
        compiler_params=pltpu.CompilerParams(vmem_limit_bytes=held_bytes + (room << 20)),
        name=getattr(kernel, "__name__", "step"),
    )(*operands, *later)


def join_parts(ways):
    def join(given_ref, *refs):
        for part, way in enumerate(ways):
            own_ref, came_ref, out_ref = refs[2 * part], refs[2 * part + 1], refs[2 * len(ways) + part]
            for rows, value in joined_rows(given_ref, way, own_ref, came_ref):
                out_ref[rows] = value

    return join


def cond_columns(given_ref, own_ref, came_ref, out_ref, rows_ref):
    for rows, value in joined_rows(given_ref, COND[1], own_ref, came_ref):
        rows_ref[rows] = value
    chip = lax.broadcasted_iota(jnp.int32, (64, 384), 0)
    latent = chip % 32 * 2 + chip // 32
    row = lax.broadcasted_iota(jnp.int32, (64, 384), 1)
    lane = lax.broadcasted_iota(jnp.int32, (128, 128), 0)
    place = lax.broadcasted_iota(jnp.int32, (128, 128), 1)
    total = jnp.zeros((64, 128), F32)
    for tile in range(6):
        values = mm(one_hot(row, 6 * latent + tile), rows_ref[...]).astype(BF)
        wanted = jnp.where(place < 6, given_ref[len(GIVEN)] * 6 + place - 128 * tile, -1)
        total += mm(values, one_hot(lane, wanted))
    out_ref[...] = total.astype(BF)


def split_parts(ways):
    def split(given_ref, *refs):
        count = len(ways)
        for part, way in enumerate(ways):
            value = refs[2 * part][...].astype(F32) + refs[2 * part + 1][...].astype(F32)
            split_rows(
                given_ref, way, value, refs[2 * count + 2 * part], refs[2 * count + 2 * part + 1]
            )

    return split


def split_all(given_ref, *refs):
    keep_ref, send_ref = refs[10], refs[11]
    at = 0
    for part, width in enumerate(BACK_WIDTHS):
        columns = slice(at, at + width)
        value = refs[2 * part][...].astype(F32) + refs[2 * part + 1][...].astype(F32)
        split_rows(given_ref, ("zl", 1, 48), value, keep_ref.at[:, columns], send_ref.at[:, columns])
        at += width


def split_last(given_ref, keep_ref, came_ref, near_keep, near_send, far_keep, far_send):
    value = keep_ref[...] + came_ref[...].astype(F32)
    second = bit_of(given_ref, "x")
    for columns, at in ((slice(0, 1152), 0), (slice(1664, 3200), 1152), (slice(1536, 1664), 2688)):
        first, last = value[:12, columns], value[12:, columns]
        to = slice(at, at + first.shape[1])
        near_keep[:, to] = jnp.where(second, last, first)
        near_send[:, to] = jnp.where(second, first, last)
    first, last = value[:, 3200:3968], value[:, 3968:]
    far_keep[:24] = jnp.where(second, last, first)
    far_send[:24] = jnp.where(second, first, last)
    for half in range(2):
        first, last = [value[12 * half + x : 12 * half + x + 6, 1152:1536] for x in (0, 6)]
        to = slice(384 * half, 384 * half + 384)
        far_keep[24:, to] = jnp.where(second, last, first)
        far_send[24:, to] = jnp.where(second, first, last)


def split_cores(given_ref, keep_ref, came_ref, far_ref, far_came_ref, near_keep, near_send, down_ref, proj_ref):
    value = keep_ref[...] + came_ref[...]
    second = bit_of(given_ref, "c")
    near_keep[...] = jnp.where(second, value[6:], value[:6])
    near_send[...] = jnp.where(second, value[:6], value[6:])
    far = far_ref[...] + far_came_ref[...]
    down_ref[...] = far[:24]
    proj_ref[...] = far[24:]


def ada_grads(core_ref, mod_ref, cond_ref, rows_ref, keep_ref, send_ref, term_ref, sums_ref):
    mods = mod_ref[...].astype(F32)
    mods = jnp.concatenate([mods[:, row, :] for row in range(18)], axis=1).astype(BF)
    pair = mm_tn(cond_ref[...], mods)
    second = bit_of(core_ref, "c")
    keep_ref[...] = jnp.where(second, pair[6:], pair[:6])
    send_ref[...] = jnp.where(second, pair[:6], pair[6:])
    term_ref[...] = mm_nt(mods, rows_ref[...])
    sums_ref[...] = column_sum(mods.astype(F32))


def one_hot(index, at):
    return (index == at).astype(F32).astype(BF)


def row_picks():
    row = lax.broadcasted_iota(jnp.int32, (768, 128), 0)
    device = lax.broadcasted_iota(jnp.int32, (768, 128), 1)
    return one_hot(row, 6 * device)


def bias_vector(units, table_ref):
    rows = mm_tn(row_picks(), units).astype(BF)
    index = lax.broadcasted_iota(jnp.int32, (128, 3840), 0)
    picked = mm_tn(rows, one_hot(index, table_ref[0:1]))
    return column_sum(jnp.where(index == table_ref[1:2], picked, 0.0))


def bias_units(vector, table_ref):
    index = lax.broadcasted_iota(jnp.int32, (128, 3840), 0)
    spread_out = jnp.where(index == table_ref[0:1], vector, 0.0).astype(BF)
    rows = mm_nt(spread_out, one_hot(index, table_ref[1:2])).astype(BF)
    return mm(row_picks(), rows)


def copy_of(value_ref, out_ref):
    out_ref[...] = value_ref[...]


def mod_add(keep_ref, came_ref, out_ref):
    total = keep_ref[...] + came_ref[...]
    for row in range(18):
        out_ref[:, row, :] = total[:, 128 * row : 128 * row + 128]


def mod_sum(got_ref, out_ref):
    total = jnp.sum(got_ref[...], axis=0)
    for row in range(18):
        at = 128 * (row % 6)
        out_ref[row // 6 : row // 6 + 1, at : at + 128] = total[row : row + 1]


def mod_grads(core_ref, start_ref, middle_ref, out_ref, keep_ref, send_ref):
    first = jnp.concatenate([start_ref[...], middle_ref[0:1]], axis=0)
    last = jnp.concatenate([middle_ref[1:3], out_ref[0:1]], axis=0)
    second = core_ref[0] == 1
    keep_ref[...] = jnp.where(second, last, first)
    send_ref[...] = jnp.where(second, first, last)


def mod_join(keep_ref, came_ref, out_ref):
    total = keep_ref[...] + came_ref[...]
    rows = [
        total[row // 6 : row // 6 + 1, 128 * (row % 6) : 128 * (row % 6) + 128] for row in range(18)
    ]
    out_ref[...] = jnp.broadcast_to(jnp.concatenate(rows, axis=0)[None], (64, 18, 128)).astype(BF)


def owners(core_ref, keep_ref, came_ref, qkv_ref, qv_ref, proj_ref, up_ref, up_bias_ref, down_ref):
    keep, came = keep_ref[...], came_ref[...]
    second = core_ref[0] == 1
    left, right = jnp.where(second, came, keep), jnp.where(second, keep, came)
    for part in range(3):
        from_ = slice(384 * part, 384 * part + 384)
        for row in range(6):
            qkv_ref[row, :, 768 * part : 768 * part + 384] = left[row : row + 1, from_]
            qkv_ref[row, :, 768 * part + 384 : 768 * part + 768] = right[row : row + 1, from_]
    for row in range(6):
        up_ref[row, :, :1536] = left[row : row + 1, 1152:2688]
        up_ref[row, :, 1536:] = right[row : row + 1, 1152:2688]
    sums = (keep + came)[0:1, 2688:]
    qv_ref[...] = sums[:, :12]
    up_bias_ref[...] = sums[:, 12:36]
    proj_ref[...] = sums[:, 36:42]
    down_ref[...] = sums[:, 42:48]


def part_ways(core_ref, value, keep_ref, send_ref):
    second = core_ref[0] == 1
    keep_ref[...] = jnp.where(second, value[128:], value[:128])
    send_ref[...] = jnp.where(second, value[:128], value[128:])


def modulate(normed, mod_ref, shift):
    return (normed * (1.0 + mod_ref[shift + 1 : shift + 2]) + mod_ref[shift : shift + 1]).astype(BF)


def column_sum(value):
    return jnp.sum(value, axis=0, keepdims=True)


def first_mix(x_ref, mod_ref, mixed_ref):
    normed, _ = normalize(x_ref[...].astype(F32))
    mixed_ref[...] = modulate(normed, mod_ref, 0)


def attend(
    core_ref, mixed_ref, own_ref, came_ref, bias_table_ref, table_ref,
    bias_ref, weight_ref, qkv_ref, attended_ref, proj_ref, keep_ref, send_ref,
):
    for rows, value in joined_rows(core_ref, OUT[0][2], own_ref, came_ref):
        weight_ref[rows] = value
    bias_ref[...] = bias_vector(weight_ref[:, 1536:], bias_table_ref)
    projected = mm(mixed_ref[...], weight_ref[:, :1152])
    qkv_ref[:, :384] = (projected[:, :384] + bias_ref[:, :384]).astype(BF)
    qkv_ref[:, 384:768] = projected[:, 384:768].astype(BF)
    qkv_ref[:, 768:] = (projected[:, 768:] + bias_ref[:, 384:768]).astype(BF)
    units = weight_ref[:, 1152:1536]
    index = lax.broadcasted_iota(jnp.int32, (384, 768), 1)
    for half in range(2):
        picks = one_hot(index, table_ref[:, half : half + 1])
        proj_ref[:, 384 * half : 384 * half + 384] = mm(picks, units).astype(BF)
    for head in range(6):
        query, keys, values = head_cuts(qkv_ref, head)
        probs = soft_probs(query, keys).astype(BF)
        at = head * HEAD_DIM
        attended_ref[:, at : at + HEAD_DIM] = mm(probs, values).astype(BF)
    part_ways(core_ref, mm(attended_ref[...], proj_ref[...]), keep_ref, send_ref)


def second_mix(keep_ref, came_ref, bias_ref, x_ref, mod_ref, branch_ref, middle_ref, mixed_ref):
    branch = keep_ref[...] + came_ref[...] + bias_ref[:, 2304:3072]
    middle = x_ref[...].astype(F32) + mod_ref[2:3] * branch
    normed, _ = normalize(middle)
    branch_ref[...] = branch
    middle_ref[...] = middle
    mixed_ref[...] = modulate(normed, mod_ref, 3)


def down_rows(pair, half):
    return [(2 * pair + side) * 96 + half * 48 for side in range(2)]


def feed(
    core_ref, mixed_ref, grad_ref, bias_ref, up_own_ref, up_came_ref, own_ref, came_ref,
    keep_ref, send_ref, back_keep_ref, back_send_ref,
    a_keep_ref, a_send_ref, b_keep_ref, b_send_ref, c_keep_ref, c_send_ref, sums_ref,
    hidden_ref, slope_ref, down_ref, up_ref, units_ref,
):
    for rows, value in joined_rows(core_ref, OUT[1][2], up_own_ref, up_came_ref):
        up_ref[rows] = value
    for rows, value in joined_rows(core_ref, OUT[2][2], own_ref, came_ref):
        units_ref[rows] = value
    mixed, grad = mixed_ref[...], grad_ref[...]
    for at in range(0, 1536, 512):
        pre = mm(mixed, up_ref[:, at : at + 512]) + bias_ref[:, 768 + at : 1280 + at]
        square = pre * pre
        tanh = jnp.tanh(0.7978845608028654 * pre * (1.0 + 0.044715 * square))
        half = 0.5 * (1.0 + tanh)
        hidden_ref[:, at : at + 512] = (pre * half).astype(BF)
        slope_ref[:, at : at + 512] = half + 0.5 * pre * (1.0 - tanh * tanh) * (
            0.7978845608028654 * (1.0 + 3.0 * 0.044715 * square)
        )
    for pair in range(8):
        for half in range(2):
            columns = slice(half * 768, half * 768 + 768)
            near = units_ref[48 * pair : 48 * pair + 48, columns].astype(F32)
            far = units_ref[384 + 48 * pair : 432 + 48 * pair, columns].astype(F32)
            for side, row in enumerate(down_rows(pair, half)):
                cut_ = slice(24 * side, 24 * side + 24)
                down_ref[row : row + 48] = jnp.concatenate([near[cut_], far[cut_]]).astype(BF)
    hidden, down = hidden_ref[...], down_ref[...]
    grad_pre = (mm_nt(grad, down) * slope_ref[...]).astype(BF)
    part_ways(core_ref, mm_nt(grad_pre, up_ref[...]), back_keep_ref, back_send_ref)
    part_ways(core_ref, mm(hidden, down), keep_ref, send_ref)
    grad_up = mm_tn(mixed, grad_pre)
    split_rows(core_ref, BACK[2][0], grad_up[:, :1024], a_keep_ref, a_send_ref)
    grad_down = mm_tn(hidden, grad)
    for pair in range(8):
        for half in range(2):
            columns = slice(half * 768, half * 768 + 768)
            for side in range(2):
                units_ref[384 * side + 48 * pair : 384 * side + 48 * pair + 48, columns] = jnp.concatenate(
                    [grad_down[r + 24 * side : r + 24 * side + 24] for r in down_rows(pair, half)]
                ).astype(BF)
    left, right = slice(0, 512), slice(512, 1024)
    split_rows(core_ref, BACK[3][0], grad_up[:, 1024:], b_keep_ref.at[:, left], b_send_ref.at[:, left])
    split_rows(core_ref, BACK[3][0], units_ref[:, :512], b_keep_ref.at[:, right], b_send_ref.at[:, right])
    split_rows(core_ref, BACK[4][0], units_ref[:, 512:], c_keep_ref, c_send_ref)
    sums_ref[...] = column_sum(grad_pre.astype(F32))


def finish(keep_ref, came_ref, bias_ref, middle_ref, grad_ref, mod_ref, out_ref, sums_ref):
    branch = keep_ref[...] + came_ref[...] + bias_ref[:, 3072:3840]
    out_ref[...] = (middle_ref[...] + mod_ref[5:6] * branch).astype(BF)
    grad = grad_ref[...].astype(F32)
    sums_ref[0:1] = column_sum(grad * branch)
    sums_ref[1:2] = column_sum((mod_ref[5:6] * grad).astype(BF).astype(F32))


def middle_back(
    keep_ref, came_ref, middle_ref, branch_ref, grad_ref, mod_ref, grad_middle_ref, grad_branch_ref, sums_ref
):
    grad_mixed = keep_ref[...] + came_ref[...]
    normed, recip = normalize(middle_ref[...])
    grad_middle = grad_ref[...].astype(F32) + norm_back(
        grad_mixed * (1.0 + mod_ref[4:5]), normed, recip
    )
    grad_branch = (mod_ref[2:3] * grad_middle).astype(BF)
    grad_middle_ref[...] = grad_middle
    grad_branch_ref[...] = grad_branch
    sums_ref[0:1] = column_sum(grad_middle * branch_ref[...])
    sums_ref[1:2] = column_sum(grad_mixed)
    sums_ref[2:3] = column_sum(grad_mixed * normed)
    sums_ref[3:4] = column_sum(grad_branch.astype(F32))


def attend_back(
    core_ref, grad_ref, proj_ref, qkv_ref, attended_ref, mixed_ref, weight_ref,
    table_ref, bias_table_ref, up_sums_ref, middle_sums_ref, out_sums_ref,
    keep_ref, send_ref, one_keep_ref, one_send_ref, two_keep_ref, two_send_ref, grad_qkv_ref,
):
    grad = grad_ref[...]
    grad_attended = mm_nt(grad, proj_ref[...]).astype(BF)
    for head in range(6):
        query, keys, values = head_cuts(qkv_ref, head)
        at = head * HEAD_DIM
        grad_out = grad_attended[:, at : at + HEAD_DIM]
        probs = soft_probs(query, keys)
        grad_probs = mm_nt(grad_out, values)
        total = jnp.sum(probs * grad_probs, axis=-1, keepdims=True)
        grad_scores = (probs * (grad_probs - total)).astype(BF)
        grad_qkv_ref[:, at : at + HEAD_DIM] = (mm(grad_scores, keys) * 0.125).astype(BF)
        at += 384
        grad_qkv_ref[:, at : at + HEAD_DIM] = (mm_tn(grad_scores, query) * 0.125).astype(BF)
        at += 384
        grad_qkv_ref[:, at : at + HEAD_DIM] = mm_tn(probs.astype(BF), grad_out).astype(BF)
    grad_qkv = grad_qkv_ref[...]
    part_ways(core_ref, mm_nt(grad_qkv, weight_ref[:, :1152]), keep_ref, send_ref)
    one = mm_tn(mixed_ref[...], grad_qkv[:, :768])
    split_rows(core_ref, BACK[0][0], one, one_keep_ref, one_send_ref)
    grad_proj = mm_tn(attended_ref[...], grad).astype(BF)
    index = lax.broadcasted_iota(jnp.int32, (384, 768), 1)
    units = jnp.zeros((768, 384), F32)
    for half in range(2):
        picks = one_hot(index, table_ref[:, half : half + 1])
        units += mm_tn(picks, grad_proj[:, 384 * half : 384 * half + 384])
    sums = column_sum(grad_qkv.astype(F32))
    vector = jnp.concatenate(
        [sums[:, :384], sums[:, 768:], up_sums_ref[...], middle_sums_ref[3:4], out_sums_ref[1:2]], axis=1
    )
    two = jnp.concatenate(
        [mm_tn(mixed_ref[...], grad_qkv[:, 768:]), units, bias_units(vector, bias_table_ref)], axis=1
    )
    split_rows(core_ref, BACK[1][0], two, two_keep_ref, two_send_ref)


def start_back(keep_ref, came_ref, x_ref, grad_middle_ref, mod_ref, grad_ref, sums_ref):
    grad_mixed = keep_ref[...] + came_ref[...]
    normed, recip = normalize(x_ref[...].astype(F32))
    grad_ref[...] = grad_middle_ref[...] + norm_back(
        grad_mixed * (1.0 + mod_ref[1:2]), normed, recip
    )
    sums_ref[0:1] = column_sum(grad_mixed)
    sums_ref[1:2] = column_sum(grad_mixed * normed)


def body(
    latents_in,
    condition,
    ada_weight,
    ada_bias,
    qkv_weight,
    qv_bias,
    proj_weight,
    proj_bias,
    fc1_weight,
    fc1_bias,
    fc2_weight,
    fc2_bias,
    cotangent,
):
    core = lax.axis_index("c")
    at_s = lax.axis_index("s")
    cond = condition.astype(F32)
    cond_low = jax.nn.silu(cond).astype(BF)

    qkv_cut = qkv_weight[0].reshape(6, 3, 2, 384)
    bias_row = jnp.concatenate([qv_bias, fc1_bias, proj_bias, fc2_bias], axis=1)
    bias_tile = jnp.pad(bias_row, ((0, 5), (0, 128 - 48)))
    first = jnp.concatenate([qkv_cut[:, :, 0].reshape(6, 1152), fc1_weight[0, :, :1536]], axis=1)
    last = jnp.concatenate([qkv_cut[:, :, 1].reshape(6, 1152), fc1_weight[0, :, 1536:]], axis=1)
    mine, theirs = halves(first, last, "c")
    tiles = jnp.concatenate([bias_tile, cond_low.reshape(6, 128)], axis=1)
    mine = jnp.concatenate([mine, tiles], axis=1)
    theirs = jnp.concatenate([theirs, tiles], axis=1)
    other = swap(theirs, "c")
    second = core == 1
    unit12 = jnp.concatenate(
        [jnp.where(second, other, mine), jnp.where(second, mine, other)], axis=0
    )
    unit24 = pair_up(unit12, "x", 0)
    crossed = cross(jnp.concatenate([fc2_weight[0], proj_weight[0]], axis=0))
    crossed = pair_up(crossed[None], "x", 0)
    proj_unit = crossed[:, 24:].reshape(2, 6, 2, 384).transpose(2, 0, 1, 3).reshape(24, 384)
    unit = jnp.concatenate(
        [unit24[:, :1152], proj_unit, unit24[:, 2688:2816], unit24[:, 1152:2688], crossed[0, :24], crossed[1, :24], unit24[:, 2816:]],
        axis=1,
    )
    near = pair_up(pair_up(unit[None], "yl", 0)[None], "zl", 0).reshape(96, 4864)

    which = jnp.stack([lax.axis_index(a) for a in (*GIVEN, NAMES)]).astype(jnp.int32)

    def step_out(parts, ways, later=()):
        pairs = [x for p, way in zip(parts, ways) for x in (p, swap(p, way[0]))]
        shapes = [((p.shape[0] * 2, p.shape[1]), BF) for p in parts]
        return call(join_parts(ways), shapes, which, *pairs, later=later)

    *parts, conds = step_out(cut(near, (*WIDTHS, 128)), [*(way[0] for way in OUT), COND[0]])
    (cond_cols,) = call(
        cond_columns, [((64, 128), BF)], which, conds, swap(conds, "zh"),
        scratch=[pltpu.VMEM((384, 128), BF)],
    )
    cond_cols = cond_cols[:, :6]
    pair_cond = pair_up(cond_cols, "c", 1)

    device = lax.axis_index(NAMES)
    own_bias = lax.dynamic_update_slice(jnp.zeros((4608,), F32), ada_bias[0].astype(F32), (device * 36,))
    partial = mm(cond_cols, ada_weight[0]) + own_bias
    keep, send = halves(partial[:, :2304], partial[:, 2304:], "c")
    (partial,) = call(mod_add, [((64, 18, 128), F32)], keep, swap(send, "c"))
    mod_parts = exchange(partial, CHIPS)
    one = step_out(parts[:1], [OUT[0][1]])
    parts = [*one, *step_out(parts[1:], [way[1] for way in OUT[1:]], (mod_parts,))]
    (mod_half,) = call(mod_sum, [((3, 768), F32)], mod_parts)
    modulation = lax.all_gather(mod_half, "c", axis=0, tiled=True)

    one_own, up_own, units_own = parts
    one_came, up_came, units_came = [swap(p, way[2][0]) for p, way in zip(parts, OUT)]

    proj_rows = jnp.asarray(proj_table())
    bias_places = lax.dynamic_index_in_dim(jnp.asarray(bias_table()), core, 0, False)
    resid, grad_out = cross(latents_in[0]), cross(cotangent[0])
    own = ((128, 768), F32)
    own_low = ((128, 768), BF)
    (mixed_a,) = call(first_mix, [own_low], resid, modulation)
    mixed_a = lax.all_gather(mixed_a, "c", axis=0, tiled=True)
    own_gbb = (modulation[5:6] * grad_out.astype(F32)).astype(BF)
    grad_branch_b = lax.all_gather(own_gbb, "c", axis=0, tiled=True)
    biases, weight_one, qkv, attended, proj_half, keep, send = call(
        attend,
        [((1, 3840), F32), ((768, 1664), BF), ((256, 1152), BF), ((256, 384), BF), ((384, 768), BF), own, own],
        which, mixed_a, one_own, one_came, bias_places, proj_rows,
        room=10,
        later=(grad_branch_b,),
    )
    branch_a, middle, mixed_b = call(
        second_mix, [own, own, own_low], keep, swap(send, "c"), biases, resid, modulation
    )
    mixed_b = lax.all_gather(mixed_b, "c", axis=0, tiled=True)
    out_keep, out_send, keep, send, *feed_parts, up_sums = call(
        feed,
        [own] * 4 + [((384, 1024), BF)] * 6 + [((1, 1536), F32)],
        which, mixed_b, grad_branch_b, biases, up_own, up_came, units_own, units_came,
        scratch=[
            pltpu.VMEM((256, 1536), BF),
            pltpu.VMEM((256, 1536), F32),
            pltpu.VMEM((1536, 768), BF),
            pltpu.VMEM((768, 1536), BF),
            pltpu.VMEM((768, 1536), BF),
        ],
        room=30,
    )
    grad_middle, own_gba, middle_sums = call(
        middle_back,
        [own, own_low, ((4, 768), F32)],
        keep, swap(send, "c"), middle, branch_a, grad_out, modulation,
    )
    grad_branch_a = lax.all_gather(own_gba, "c", axis=0, tiled=True)
    output, out_sums = call(
        finish,
        [own_low, ((2, 768), F32)],
        out_keep, swap(out_send, "c"), biases, middle, grad_out, modulation,
    )
    def step_back(parts, chosen, step, later=()):
        pairs = [x for (k, v), i in zip(parts, chosen) for x in (k, swap(v, BACK[i][step][0]))]
        rows = 192 // (step + 1)
        shapes = [((rows, BACK_WIDTHS[i]), BF) for i in chosen for _ in range(2)]
        ways = [BACK[i][step + 1] for i in chosen]
        done = call(split_parts(ways), shapes, which, *pairs, later=later)
        return list(zip(done[::2], done[1::2]))

    feed_parts = list(zip(feed_parts[::2], feed_parts[1::2]))
    feed_parts = step_back(feed_parts, (2, 3, 4), 0)
    keep, send, one_keep, one_send, two_keep, two_send = call(
        attend_back,
        [own, own] + [((384, 768), BF)] * 2 + [((384, 896), BF)] * 2,
        which, grad_branch_a, proj_half, qkv, attended, mixed_a, weight_one,
        proj_rows, bias_places, up_sums, middle_sums, out_sums,
        scratch=[pltpu.VMEM((256, 1152), BF)],
        room=20,
    )
    grad_resid, start_sums = call(
        start_back,
        [own, ((2, 768), F32)],
        keep, swap(send, "c"), resid, grad_middle, modulation,
        later=feed_parts[0],
    )

    far_one = [(one_keep, one_send), (two_keep, two_send)]
    far_one = step_back(far_one, (0, 1), 0)
    feed_parts = step_back(feed_parts, (2, 3, 4), 1, (far_one[0][0],))
    far_two = step_back(far_one, (0, 1), 1, (feed_parts[0][0],))

    ada_keep, ada_give = halves(ada_weight[0, :, :2304], ada_weight[0, :, 2304:], "c")
    ada_came = swap(ada_give, "c")
    second = core == 1
    ada_rows = jnp.concatenate(
        [jnp.where(second, ada_came, ada_keep), jnp.where(second, ada_keep, ada_came)], axis=0
    )
    keep, send = call(
        mod_grads, [((3, 768), F32)] * 2, which, start_sums, middle_sums, out_sums
    )
    (grad_mod,) = call(mod_join, [((64, 18, 128), BF)], keep, swap(send, "c"), later=feed_parts[0])
    all_mod = exchange(grad_mod, CHIPS)
    keep, give, term, sums = call(
        ada_grads,
        [((6, 2304), F32)] * 2 + [((64, 12), F32), ((1, 2304), F32)],
        which, all_mod, pair_cond, ada_rows,
    )
    came = swap(give, "c")
    grad_ada = jnp.concatenate(
        [jnp.where(second, came, keep), jnp.where(second, keep, came)], axis=1
    )[None]
    ada_sums = jnp.where(core == at_s, sums, swap(sums, "c"))
    grad_ada_bias = lax.dynamic_slice_in_dim(ada_sums, device % 64 * 36, 36, 1)
    term = term.reshape(2, 32, 12).transpose(1, 0, 2).reshape(32, 24)
    term = exchange(jnp.concatenate([term, term], axis=0), CHIPS)

    pairs = [x for (k, v), way in zip(far_two + feed_parts, BACK) for x in (k, swap(v, way[2][0]))]
    keep, send = call(
        split_all, [((48, 4736), F32), ((48, 4736), BF)], which, *pairs
    )
    (grad_resid,) = call(copy_of, [own], grad_resid, later=(keep,))
    (output,) = call(copy_of, [own_low], output, later=(keep,))
    latents_grad, output = cross(grad_resid), cross(output)
    keep, send = call(
        split_parts([("yl", 1, 24)]), [((24, 4736), F32), ((24, 4736), BF)], which, keep, swap(send, "zl")
    )
    near_keep, near_send, far_keep, far_send = call(
        split_last,
        [((12, 2816), F32)] * 2 + [((30, 768), F32)] * 2,
        which, keep, swap(send, "yl"),
    )
    keep, send, down, proj = call(
        split_cores,
        [((6, 2816), F32)] * 2 + [((24, 768), F32), ((6, 768), F32)],
        which, near_keep, swap(near_send, "x"), far_keep, swap(far_send, "x"),
    )
    grad_fc2, grad_proj = cross(down)[None], cross(proj)[None]
    grad_qkv, grad_qv, grad_proj_bias, grad_fc1, grad_fc1_bias, grad_fc2_bias = call(
        owners,
        [((6, 1, 2304), F32), ((1, 12), F32), ((1, 6), F32), ((6, 1, 3072), F32), ((1, 24), F32), ((1, 6), F32)],
        which, keep, swap(send, "c"),
    )

    (term,) = call(copy_of, [((64, 24), F32)], term, later=(near_keep,))
    term = term.reshape(64, 2, 12).transpose(1, 0, 2).reshape(2, 768)
    cond_sum = pair_sum(term, "c", 0)
    sigmoid = jax.nn.sigmoid(cond)
    cond_grad = cond_sum * (sigmoid * (1.0 + cond * (1.0 - sigmoid)))

    return (
        output[None],
        latents_grad[None],
        cond_grad,
        grad_ada,
        grad_ada_bias,
        grad_qkv.reshape(1, 6, 2304),
        grad_qv,
        grad_proj,
        grad_proj_bias,
        grad_fc1.reshape(1, 6, 3072),
        grad_fc1_bias,
        grad_fc2,
        grad_fc2_bias,
    )


def solution(mesh):
    finer = Mesh(mesh.devices.reshape(SIZES), NAMES)
    tokens = P(NAMES[1:], "s", None)
    cond = P(NAMES[1:], None)
    matrix = P(None, NAMES, None)
    vector = P(None, NAMES)
    weights = (matrix, vector) * 5
    return jax.shard_map(
        body,
        mesh=finer,
        in_specs=(tokens, cond) + weights + (tokens,),
        out_specs=(tokens, tokens, cond) + weights,
        check_vma=False,
    )
```
